512 devices in a mesh: seq: 32 (over y_lo, z), head: 16 (over y_hi, x, core).
Axes of the slice: x: 4, y: 8 (y_hi: 2, y_lo: 4; y = y_hi * 4 + y_lo), z: 8, core: 2. Of those that a mesh axis runs over, the one named last changes fastest.
Arguments:
- queries: bfloat16 [65536, 4096], P(('seq', 'head')), may hold values from -6 to 6
- out_grad: bfloat16 [65536, 4096], P(('seq', 'head')), may hold values from -24 to 24
- latents: bfloat16 [32, 64, 1280], P('seq'), may hold values from -6 to 6
- key_weight: bfloat16 [1280, 4096], P(None, 'head'), may hold values from -0.15625 to 0.15625
- value_weight: bfloat16 [1280, 4096], P(None, 'head'), may hold values from -0.15625 to 0.15625
- query_gain: float32 [128], replicated, may hold values from 0.25 to 1.75
- key_gain: float32 [128], replicated, may hold values from 0.25 to 1.75
- gate_alpha: float32 [1], replicated, may hold values from 0.5 to 1.5
- media_slot: int32 [32], replicated, may hold values from 0 to 31, each once
- media_position: int32 [32], replicated, may hold values from 0 to 65535, as said below
- tile_list: int32 [128, 8], P('seq'), may hold values from -1 to 31, as said below
Outputs:
- grad_queries: bfloat16 [65536, 4096], P(('seq', 'head'))
- grad_latents: bfloat16 [32, 64, 1280], P('seq', 'head')
- grad_key_weight: float32 [1280, 4096], P('seq', 'head')
- grad_value_weight: float32 [1280, 4096], P('seq', 'head')
The draws below stay inside these ranges and needn't reach their ends.
Inputs may be any that keep to these rules, and one draw needn't show every extreme that they name: `tile_list`: row i names, in increasing order, consecutive image numbers: the images of tile i's document with media_position below (i + 1) * 512 - 1, then -1 in the remaining entries. Documents cover whole tiles. Every image is named by some row. `media_position`: strictly increasing in the image number; an image lies within the tokens of its document.
All inputs are finite; a program needn't handle non-finite values.
Results may differ from the reference program's by a relative error of at most 0.035.
Values may be sent and summed in bfloat16 or wider, within the bound.
A program may use at most 64 MiB of HBM per device.

```python
import jax
import jax.numpy as jnp
from jax import lax

HD = 128
VD = 1280
LAT = 64
TILE = 512
LIST = 8
TOK_DEV = 2048
IMG_DEV = 1
HEADS = 32
TOKENS = 65536
TILES = 128
IMAGES = 32
DOCS = 4
N_SEQ = 32


def doc_layout(key):
    count_key, spread_key, split_key, place_key = jax.random.split(key, 4)
    doc_range = jnp.arange(DOCS, dtype=jnp.int32)
    full_doc = jax.random.randint(count_key, (), 0, DOCS, dtype=jnp.int32)
    spare_docs = jax.random.permutation(spread_key, (DOCS - 1) * LIST).astype(jnp.int32)[:IMAGES - LIST] // LIST
    spare_docs = spare_docs + (spare_docs >= full_doc).astype(jnp.int32)
    doc_counts = jnp.sum((spare_docs[None, :] == doc_range[:, None]).astype(jnp.int32), axis=1) + LIST * (doc_range == full_doc).astype(jnp.int32)
    cut_tiles = jnp.sort(jax.random.permutation(split_key, TILES - 1).astype(jnp.int32)[:DOCS - 1] + 1)
    doc_first_tile = jnp.concatenate([jnp.zeros((1,), jnp.int32), cut_tiles])
    doc_end_tile = jnp.concatenate([cut_tiles, jnp.full((1,), TILES, jnp.int32)])
    doc_until = jnp.cumsum(doc_counts).astype(jnp.int32)
    doc_first_image = doc_until - doc_counts
    image_range = jnp.arange(IMAGES, dtype=jnp.int32)
    image_doc = jnp.sum((doc_until[None, :] <= image_range[:, None]).astype(jnp.int32), axis=1)
    image_rank = image_range - doc_first_image[image_doc]
    image_share = doc_counts[image_doc]
    span_start = doc_first_tile[image_doc] * TILE
    span_length = (doc_end_tile - doc_first_tile)[image_doc] * TILE
    segment_width = span_length // image_share
    jitter = jax.random.randint(place_key, (IMAGES,), 0, segment_width - 1, dtype=jnp.int32)
    positions = span_start + image_rank * segment_width + jitter
    tile_range = jnp.arange(TILES, dtype=jnp.int32)
    tile_doc = jnp.sum((cut_tiles[None, :] <= tile_range[:, None]).astype(jnp.int32), axis=1)
    tile_limit = (tile_range + 1) * TILE - 1
    seen_images = (image_doc[None, :] == tile_doc[:, None]) & (positions[None, :] < tile_limit[:, None])
    tile_counts = jnp.sum(seen_images.astype(jnp.int32), axis=1)
    entry_range = jnp.arange(LIST, dtype=jnp.int32)
    tile_lists = jnp.where(entry_range[None, :] < tile_counts[:, None], doc_first_image[tile_doc][:, None] + entry_range[None, :], -1)
    return (positions.astype(jnp.int32), tile_lists.astype(jnp.int32))


def draw_media_position(key, part):
    positions, tile_lists = doc_layout(key)
    return positions


def draw_tile_list(key, part):
    positions, tile_lists = doc_layout(key)
    return tile_lists


def level_of(rng, shape, cuts, low, top_value):
    def one(dim, blocks):
        heights = jax.random.uniform(jax.random.fold_in(jax.random.fold_in(rng, 6), dim), (blocks,), jnp.float32, low / len(cuts), top_value / len(cuts))
        return jnp.repeat(jnp.exp(heights), shape[dim] // blocks).reshape((-1,) + (1,) * (len(shape) - dim - 1))

    factor_of = one(*cuts[0])
    for cut in cuts[1:]:
        factor_of = factor_of * one(*cut)
    return factor_of


def scatter_about(rng, shape, width, reach, cuts=(), held_as=jnp.bfloat16):
    values = width * jax.random.normal(rng, shape, jnp.float32)
    if cuts:
        values = values * level_of(rng, shape, cuts, -0.22, 0.18)
    return jnp.clip(values, -reach, reach).astype(held_as)


def setup_inputs(seed: int = 0) -> dict:
    keys = jax.random.split(jax.random.key(seed), 12)
    queries = scatter_about(keys[0], (TOKENS, HEADS * HD), 1.0, 6.0, ((0, 512),))
    out_grad = scatter_about(keys[1], (TOKENS, HEADS * HD), 4.0, 24.0, ((0, 512),))
    latents = scatter_about(keys[2], (IMAGES, LAT, VD), 1.0, 6.0, ((0, 32),))
    key_weight = scatter_about(keys[3], (VD, HEADS * HD), VD ** -0.5, 0.15625, ((1, 16),))
    value_weight = scatter_about(keys[4], (VD, HEADS * HD), VD ** -0.5, 0.15625, ((1, 16),))
    query_gain = jnp.clip(1.0 + 0.15 * jax.random.normal(keys[5], (HD,), jnp.float32), 0.25, 1.75)
    key_gain = jnp.clip(1.0 + 0.15 * jax.random.normal(keys[6], (HD,), jnp.float32), 0.25, 1.75)
    gate_alpha = jnp.clip(jax.random.uniform(keys[7], (1,), jnp.float32, 0.5, 1.5), 0.5, 1.5)
    media_slot = jax.random.permutation(keys[8], IMAGES).astype(jnp.int32)
    media_position = draw_media_position(jax.random.fold_in(keys[11], 71), 0)
    tile_list = draw_tile_list(jax.random.fold_in(keys[11], 71), 0)
    return dict(queries=queries, out_grad=out_grad, latents=latents, key_weight=key_weight, value_weight=value_weight, query_gain=query_gain, key_gain=key_gain, gate_alpha=gate_alpha, media_slot=media_slot, media_position=media_position, tile_list=tile_list)


EPS = 1e-06

def head_norm(raw_rows, gain_row):
    inverse = lax.rsqrt(lax.optimization_barrier(jnp.mean(raw_rows * raw_rows, axis=-1, keepdims=True)) + EPS)
    return (raw_rows * inverse * gain_row, inverse)

def norm_back(upstream, raw_rows, inverse, gain_row):
    scaled = upstream * gain_row
    row_inner = lax.optimization_barrier(jnp.mean(scaled * raw_rows, axis=-1, keepdims=True))
    return inverse * (scaled - raw_rows * inverse * inverse * row_inner)

def reference(queries, out_grad, latents, key_weight, value_weight, query_gain, key_gain, gate_alpha, media_slot, media_position, tile_list):
    scale_factor = HD ** (-0.5)
    gate_value = jnp.tanh(gate_alpha[0])
    full_width = HEADS * HD
    tiles_dev = TOK_DEV // TILE
    latent_flat = latents.reshape(IMAGES * LAT, VD)
    raw_keys = jnp.dot(latent_flat, key_weight, preferred_element_type=jnp.float32).reshape(IMAGES, LAT, HEADS, HD)
    normed, key_inverse = head_norm(raw_keys, key_gain)
    stored_keys = normed.astype(jnp.bfloat16)
    stored_values = jnp.dot(latent_flat, value_weight, preferred_element_type=jnp.float32).astype(jnp.bfloat16).reshape(IMAGES, LAT, HEADS, HD)
    keys_by_image = stored_keys[media_slot]
    values_by_image = stored_values[media_slot]
    query_blocks = queries.reshape(N_SEQ, tiles_dev, TILE, HEADS, HD)
    grad_blocks = out_grad.reshape(N_SEQ, tiles_dev, TILE, HEADS, HD)
    list_blocks = tile_list.reshape(N_SEQ, tiles_dev, LIST)

    def one_tile(inputs):
        query_tile, grad_tile, list_row, tile_start = inputs
        entry_live = list_row >= 0
        image_ids = jnp.maximum(list_row, 0)
        key_tile = keys_by_image[image_ids].reshape(LIST * LAT, HEADS, HD)
        value_tile = values_by_image[image_ids].reshape(LIST * LAT, HEADS, HD)
        image_places = media_position[image_ids]
        token_places = tile_start + jnp.arange(TILE, dtype=jnp.int32)
        entry_ok = entry_live[None, :] & (image_places[None, :] < token_places[:, None])
        key_ok = jnp.repeat(entry_ok, LAT, axis=1)
        has_key = jnp.any(entry_ok, axis=1)
        query_full = query_tile.astype(jnp.float32)
        query_hat, query_inverse = head_norm(query_full, query_gain)
        query_hat = query_hat.astype(jnp.bfloat16)
        scores = jnp.einsum('qhd,khd->hqk', query_hat.astype(jnp.float32), key_tile.astype(jnp.float32)) * scale_factor
        exp_scores = jnp.where(key_ok[None], jnp.exp(scores), 0.0)
        denominator = lax.optimization_barrier(jnp.sum(exp_scores, axis=2, keepdims=True)) + jnp.where(has_key, 0.0, 1.0)[None, :, None]
        probs = (exp_scores / denominator).astype(jnp.bfloat16)
        grad_ctx = (gate_value * grad_tile.astype(jnp.float32)).astype(jnp.bfloat16)
        grad_probs = jnp.einsum('qhd,khd->hqk', grad_ctx.astype(jnp.float32), value_tile.astype(jnp.float32))
        probs_full = probs.astype(jnp.float32)
        row_inner = lax.optimization_barrier(jnp.sum(probs_full * grad_probs, axis=2, keepdims=True))
        grad_scores = (probs_full * (grad_probs - row_inner) * scale_factor).astype(jnp.bfloat16)
        grad_qhat = jnp.einsum('hqk,khd->qhd', grad_scores.astype(jnp.float32), key_tile.astype(jnp.float32))
        grad_query = norm_back(grad_qhat, query_full, query_inverse, query_gain).astype(jnp.bfloat16)
        grad_key = jnp.einsum('hqk,qhd->khd', grad_scores.astype(jnp.float32), query_hat.astype(jnp.float32))
        grad_value = jnp.einsum('hqk,qhd->khd', probs_full, grad_ctx.astype(jnp.float32))
        return (grad_query.reshape(TILE, full_width), grad_key.reshape(LIST, LAT, HEADS, HD), grad_value.reshape(LIST, LAT, HEADS, HD))

    def one_shard(running, inputs):
        query_shard, grad_shard, list_shard, shard_index = inputs
        tile_starts = shard_index * TOK_DEV + jnp.arange(tiles_dev, dtype=jnp.int32) * TILE
        grad_queries, grad_keys, grad_values = lax.map(one_tile, (query_shard, grad_shard, list_shard, tile_starts))
        entry_slot = jnp.where(list_shard >= 0, media_slot[jnp.maximum(list_shard, 0)], IMAGES).reshape(tiles_dev * LIST).astype(jnp.int32)
        key_part = jax.ops.segment_sum(grad_keys.reshape(tiles_dev * LIST, LAT, HEADS, HD), entry_slot, num_segments=IMAGES + 1)[:IMAGES]
        value_part = jax.ops.segment_sum(grad_values.reshape(tiles_dev * LIST, LAT, HEADS, HD), entry_slot, num_segments=IMAGES + 1)[:IMAGES]
        key_part = lax.optimization_barrier(key_part.astype(jnp.bfloat16)).astype(jnp.float32)
        value_part = lax.optimization_barrier(value_part.astype(jnp.bfloat16)).astype(jnp.float32)
        return ((running[0] + key_part, running[1] + value_part), grad_queries.reshape(TOK_DEV, full_width))
    zero_grads = jnp.zeros((IMAGES, LAT, HEADS, HD), jnp.float32)
    shard_ids = jnp.arange(N_SEQ, dtype=jnp.int32)
    sums, query_grads = lax.scan(one_shard, (zero_grads, zero_grads), (query_blocks, grad_blocks, list_blocks, shard_ids))
    key_sum, value_sum = sums
    grad_queries = query_grads.reshape(TOKENS, full_width)
    raw_grad = norm_back(key_sum, raw_keys, key_inverse, key_gain).astype(jnp.bfloat16).reshape(IMAGES * LAT, full_width)
    value_grad = value_sum.astype(jnp.bfloat16).reshape(IMAGES * LAT, full_width)
    latent_term = jnp.dot(raw_grad, key_weight.T, preferred_element_type=jnp.float32) + jnp.dot(value_grad, value_weight.T, preferred_element_type=jnp.float32)
    grad_latents = latent_term.astype(jnp.bfloat16).reshape(IMAGES, LAT, VD)
    group_rows = IMG_DEV * LAT
    latent_groups = latent_flat.reshape(N_SEQ, group_rows, VD)
    grad_groups = jnp.concatenate([raw_grad, value_grad], axis=1).reshape(N_SEQ, group_rows, 2 * full_width)

    def owner_sum(running_sum, inputs):
        latent_group, grad_group = inputs
        group_part = jnp.dot(latent_group.T, grad_group, preferred_element_type=jnp.float32)
        group_part = lax.optimization_barrier(group_part.astype(jnp.bfloat16)).astype(jnp.float32)
        return (running_sum + group_part, None)
    weight_sum, unused = lax.scan(owner_sum, jnp.zeros((VD, 2 * full_width), jnp.float32), (latent_groups, grad_groups))
    return (grad_queries, grad_latents, weight_sum[:, :full_width], weight_sum[:, full_width:])
```

```python
import jax
import jax.numpy as jnp
from jax import lax
from jax.experimental import pallas as pl
from jax.experimental.pallas import tpu as pltpu
from jax.sharding import PartitionSpec as P

HD = 128
EPS = 1e-06
SCALE = HD ** (-0.5)
LOG2E = 1.4426950408889634
MESH = pl.DeviceIdType.MESH

NZ = 8
NL = 4
NY = 8
NX = 8
LAT = 64
LIST = 8
TILE = 512
TOK = 1024
OWN = 128
COLS = 256
VD = 1280
PAD = 48
SLOTS = 32
DEAD = 1 << 30

F32 = jnp.float32
BF16 = jnp.bfloat16


def dot(a, b, ca, cb):
    return lax.dot_general(a, b, (((ca,), (cb,)), ((), ())), preferred_element_type=F32)


class Place:
    def __init__(self):
        self.seq = lax.axis_index("seq")
        self.head = lax.axis_index("head")
        self.z = lax.rem(self.seq, NZ)
        self.yl = lax.div(self.seq, NZ)
        self.yh = lax.div(self.head, NX)
        self.xc = lax.rem(self.head, NX)
        self.y = self.yh * NL + self.yl

    def at_y(self, step):
        y = lax.rem(self.y + (step + NY), NY)
        return (lax.rem(y, NL) * NZ + self.z, lax.div(y, NL) * NX + self.xc)

    def at_z(self, step):
        z = lax.rem(self.z + (step + NZ), NZ)
        return (self.yl * NZ + z, self.head)

    def at_x(self, step):
        return (self.seq, self.yh * NX + lax.rem(self.xc + step, NX))

    def at_head(self, step):
        return (self.seq, lax.rem(self.head + step, 2 * NX))

    def at_low(self, step):
        return (lax.rem(self.yl + step, NL) * NZ + self.z, self.head)


def greet(partners):
    barrier = pltpu.get_barrier_semaphore()
    for partner in partners:
        pl.semaphore_signal(barrier, inc=1, device_id=partner, device_id_type=MESH)
    pl.semaphore_wait(barrier, len(partners))


def remote(src, dst, sends, recvs, sem, device):
    return pltpu.make_async_remote_copy(
        src_ref=src,
        dst_ref=dst,
        send_sem=sends.at[sem],
        recv_sem=recvs.at[sem],
        device_id=device,
        device_id_type=MESH,
    )


class GatherRing:
    def __init__(self, block, me, right, left, sends, recvs, base):
        self.block, self.me, self.targets = block, me, (right, left)
        self.sends, self.recvs, self.base = sends, recvs, base
        self.started = []

    def copy(self, way, step, shift):
        offset = (-step - shift) if way == 0 else (step + shift)
        ref = self.block(lax.rem(self.me + (offset + 8), 8), way if step == 3 else None)
        return remote(ref, ref, self.sends, self.recvs, self.base + way * 4 + step, self.targets[way])

    def start(self, step):
        for way in (0, 1):
            copy = self.copy(way, step, 0)
            copy.start()
            self.started.append(copy)

    def wait(self, step):
        for way in (0, 1):
            self.copy(way, step, 1).wait_recv()

    def finish(self):
        for copy in self.started:
            copy.wait_send()


class ReduceRing:
    def __init__(self, own, inbox, me, right, left, sends, recvs, base):
        self.own, self.inbox, self.me, self.targets = own, inbox, me, (right, left)
        self.sends, self.recvs, self.base = sends, recvs, base
        self.started = []

    def index(self, way, step):
        offset = 4 - step if way == 0 else step + 4
        return lax.rem(self.me + offset, 8)

    def send(self, way, step, src):
        copy = remote(
            src, self.inbox(way, step), self.sends, self.recvs, self.base + way * 4 + step, self.targets[way]
        )
        copy.start()
        self.started.append(copy)

    def arrive(self, way, step):
        ref = self.inbox(way, step)
        remote(ref, ref, self.sends, self.recvs, self.base + way * 4 + step, self.targets[way]).wait_recv()

    def start(self):
        for way in (0, 1):
            self.send(way, 0, self.own(self.index(way, 0), way))

    def step(self, step):
        for way in (0, 1):
            self.arrive(way, step - 1)
            index = self.index(way, step)
            here = self.inbox(way, step - 1)
            if step == 1:
                part = self.own(index, way)
                part[...] = (part[...].astype(F32) + here[...].astype(F32)).astype(BF16)
                self.send(way, 1, self.own(index, None))
            else:
                here[...] = (here[...].astype(F32) + self.own(index, None)[...].astype(F32)).astype(BF16)
                self.send(way, step, here)

    def total(self):
        for way in (0, 1):
            self.arrive(way, 3)
        return (
            self.own(self.me, None)[...].astype(F32)
            + self.inbox(0, 3)[...].astype(F32)
            + self.inbox(1, 3)[...].astype(F32)
        )

    def finish(self):
        for copy in self.started:
            copy.wait_send()


def halves(ref, size, half):
    return ref if half is None else ref.at[pl.ds(half * size, size)]


def gather_kernel(
    queries, out_grad, latents, key_weight, value_weight, key_gain,
    q_rows, g_rows, keys, values, raw_out,
    ring_send, ring_recv, swap_send, swap_recv, local_sem,
):
    me = Place()
    greet([me.at_y(1), me.at_y(-1), me.at_z(1), me.at_z(-1)] + [me.at_x(d) for d in range(1, NX)])

    flat = latents[...]
    raw = jnp.dot(flat, key_weight[...], preferred_element_type=F32)
    raw_out[...] = raw
    for h in range(2):
        part = raw[:, h * HD:(h + 1) * HD]
        inverse = lax.rsqrt(jnp.mean(part * part, axis=1, keepdims=True) + EPS)
        keys[me.y, me.z, :, h * HD:(h + 1) * HD] = (part * inverse * key_gain[...]).astype(BF16)
    values[me.z, me.y] = jnp.dot(flat, value_weight[...], preferred_element_type=F32).astype(BF16)

    half_row = LAT // 2
    key_z = GatherRing(
        lambda b, half: halves(keys.at[me.y, b], half_row, half),
        me.z, me.at_z(1), me.at_z(-1), ring_send, ring_recv, 0)
    value_y = GatherRing(
        lambda b, half: halves(values.at[me.z, b], half_row, half),
        me.y, me.at_y(1), me.at_y(-1), ring_send, ring_recv, 8)
    key_y = GatherRing(
        lambda b, half: halves(keys.at[b], NZ // 2, half),
        me.y, me.at_y(1), me.at_y(-1), ring_send, ring_recv, 16)
    value_z = GatherRing(
        lambda b, half: halves(values.at[b], NY // 2, half),
        me.z, me.at_z(1), me.at_z(-1), ring_send, ring_recv, 24)

    key_z.start(0)
    value_y.start(0)

    swaps = []
    own = []
    for d in range(NX):
        to = lax.rem(me.xc + d, NX)
        rows = pl.ds(pl.multiple_of(me.xc * OWN, OWN), OWN)
        for n, (src, dst) in enumerate(((queries, q_rows), (out_grad, g_rows))):
            for c in range(2):
                cols = pl.ds(pl.multiple_of(c * NX * COLS + to * COLS, COLS), COLS)
                if d == 0:
                    copy = pltpu.make_async_copy(src.at[:, cols], dst.at[c, rows], local_sem.at[n * 2 + c])
                    own.append(copy)
                else:
                    copy = remote(
                        src.at[:, cols], dst.at[c, rows], swap_send, swap_recv,
                        (d - 1) * 4 + n * 2 + c, me.at_x(d))
                    swaps.append(copy)
                copy.start()

    for step in range(4):
        for first in (key_z, value_y):
            first.wait(step)
            if step < 3:
                first.start(step + 1)
    key_y.start(0)
    value_z.start(0)
    for step in range(4):
        for second in (key_y, value_z):
            second.wait(step)
            if step < 3:
                second.start(step + 1)

    for d in range(1, NX):
        source = lax.rem(me.xc + (NX - d), NX)
        rows = pl.ds(pl.multiple_of(source * OWN, OWN), OWN)
        for n, dst in enumerate((q_rows, g_rows)):
            for c in range(2):
                place = dst.at[c, rows]
                remote(place, place, swap_send, swap_recv, (d - 1) * 4 + n * 2 + c, me.at_x(d)).wait_recv()
    for copy in own:
        copy.wait()
    for copy in swaps:
        copy.wait_send()
    for ring in (key_z, value_y, key_y, value_z):
        ring.finish()


def attend_kernel(
    entry_key, entry_value, entry_place, slot_entry, first_token, gate,
    q_rows, g_rows, keys, values, query_gain,
    grad_q, grad_keys, grad_values,
    key_tile, value_tile, key_sums, value_sums,
):
    gate_value = gate[0]
    gain = query_gain[...]
    for t in range(2):
        for c in range(2):
            key_sums[t, c, LIST] = jnp.zeros((LAT, COLS), F32)
            value_sums[t, c, LIST] = jnp.zeros((LAT, COLS), F32)

    half = 256
    for t in range(2):
        for c in range(2):
            for e in range(LIST):
                rows = slice(e * LAT, (e + 1) * LAT)
                key_tile[rows, :] = keys[c * SLOTS + entry_key[t, e]]
                value_tile[rows, :] = values[c * NL + entry_value[t, e]]
            for h in range(2):
                cols = slice(h * HD, (h + 1) * HD)
                kt = key_tile[:, cols]
                vt = value_tile[:, cols]
                kt_t = kt.T
                for part in range(2):
                    base = t * TILE + part * half
                    q = q_rows[c, base:base + half, cols].astype(F32)
                    g = g_rows[c, base:base + half, cols].astype(F32)
                    inverse = lax.rsqrt(jnp.mean(q * q, axis=1, keepdims=True) + EPS)
                    q_hat = (q * inverse * gain).astype(BF16)
                    ctx = (gate_value * g).astype(BF16)
                    scores = dot(kt, q_hat, 1, 1)
                    grad_probs = dot(vt, ctx, 1, 1)
                    token = first_token[0] + base + lax.broadcasted_iota(jnp.int32, (1, half), 1)
                    total = jnp.zeros((1, half), F32)
                    inner = jnp.zeros((1, half), F32)
                    dead = jnp.ones((1, half), F32)
                    exps = []
                    for e in range(LIST):
                        rows = slice(e * LAT, (e + 1) * LAT)
                        live = entry_place[t, e] < token
                        dead = jnp.where(live, 0.0, dead)
                        x = jnp.where(live, jnp.exp2(scores[rows] * (SCALE * LOG2E)), 0.0)
                        exps.append(x)
                        total = total + jnp.sum(x, axis=0, keepdims=True)
                        inner = inner + jnp.sum(x * grad_probs[rows], axis=0, keepdims=True)
                    norm = 1.0 / (total + dead)
                    inner = inner * norm
                    probs = []
                    grads = []
                    for e in range(LIST):
                        rows = slice(e * LAT, (e + 1) * LAT)
                        p = exps[e] * norm
                        probs.append(p.astype(BF16))
                        grads.append((p * (grad_probs[rows] - inner)).astype(BF16))
                    probs = jnp.concatenate(probs, axis=0)
                    grads = jnp.concatenate(grads, axis=0)
                    dk = dot(grads, q_hat, 1, 0) * SCALE
                    dv = dot(probs, ctx, 1, 0)
                    up = dot(kt_t, grads, 1, 0).T * SCALE * gain
                    row_inner = jnp.mean(up * q, axis=1, keepdims=True)
                    grad_q[c, base:base + half, cols] = (
                        inverse * (up - q * (inverse * inverse * row_inner))
                    ).astype(BF16)
                    for e in range(LIST):
                        rows = slice(e * LAT, (e + 1) * LAT)
                        if part == 0:
                            key_sums[t, c, e, :, cols] = dk[rows]
                            value_sums[t, c, e, :, cols] = dv[rows]
                        else:
                            key_sums[t, c, e, :, cols] += dk[rows]
                            value_sums[t, c, e, :, cols] += dv[rows]

    def one_slot(s, carry):
        first = slot_entry[0, s]
        second = slot_entry[1, s]
        z = lax.rem(s, NZ)
        low = lax.div(s, NZ)
        for c in range(2):
            grad_keys[c * NL + low, z] = (key_sums[0, c, first] + key_sums[1, c, second]).astype(BF16)
            grad_values[z, c * NL + low] = (value_sums[0, c, first] + value_sums[1, c, second]).astype(BF16)
        return carry

    lax.fori_loop(0, SLOTS, one_slot, 0)


def reduce_kernel(
    grad_q, grad_keys_in, grad_values_in, raw, key_gain, key_weight, value_weight, latents_t,
    out_queries, out_latents, out_key_weight, out_value_weight,
    grad_keys, grad_values, key_in, value_in, key_mid, value_mid, key_low, value_low,
    shares, shares_in, spread, wide, weights, weights_in, low_out, low_in,
    load_sem, ring_send, ring_recv, swap_send, swap_recv, own_sem, head_send, head_recv, low_send, low_recv,
):
    me = Place()
    load_keys = pltpu.make_async_copy(grad_keys_in, grad_keys, load_sem.at[0])
    load_values = pltpu.make_async_copy(grad_values_in, grad_values, load_sem.at[1])
    load_keys.start()
    load_values.start()
    greet(
        [me.at_y(1), me.at_y(-1), me.at_z(1), me.at_z(-1)]
        + [me.at_head(d) for d in range(1, 2 * NX)]
        + [me.at_x(d) for d in range(1, NX)]
        + [me.at_low(d) for d in range(1, NL)]
    )
    load_keys.wait()
    load_values.wait()

    def inbox(buffer, size):
        def place(way, step):
            ref = buffer.at[way, step]
            return ref.at[pl.ds(way * size, size)] if step == 0 else ref
        return place

    key_y = ReduceRing(
        lambda b, half: halves(grad_keys.at[b], NZ // 2, half), inbox(key_in, NZ // 2),
        me.y, me.at_y(1), me.at_y(-1), ring_send, ring_recv, 0)
    value_z = ReduceRing(
        lambda b, half: halves(grad_values.at[b], NY // 2, half), inbox(value_in, NY // 2),
        me.z, me.at_z(1), me.at_z(-1), ring_send, ring_recv, 8)
    key_z = ReduceRing(
        lambda b, half: halves(key_mid.at[b], LAT // 2, half), inbox(key_low, LAT // 2),
        me.z, me.at_z(1), me.at_z(-1), ring_send, ring_recv, 16)
    value_y = ReduceRing(
        lambda b, half: halves(value_mid.at[b], LAT // 2, half), inbox(value_low, LAT // 2),
        me.y, me.at_y(1), me.at_y(-1), ring_send, ring_recv, 24)

    key_y.start()
    value_z.start()

    swaps = []
    own = []
    cols_of = lambda c, place: pl.ds(pl.multiple_of(c * NX * COLS + place * COLS, COLS), COLS)
    for d in range(NX):
        to = lax.rem(me.xc + d, NX)
        rows = pl.ds(pl.multiple_of(to * OWN, OWN), OWN)
        for c in range(2):
            src = grad_q.at[c, rows]
            dst = out_queries.at[:, cols_of(c, me.xc)]
            if d == 0:
                copy = pltpu.make_async_copy(src, dst, own_sem.at[c])
                own.append(copy)
            else:
                copy = remote(src, dst, swap_send, swap_recv, (d - 1) * 2 + c, me.at_x(d))
                swaps.append(copy)
            copy.start()

    for step in range(1, 4):
        key_y.step(step)
        value_z.step(step)
    key_mid[...] = key_y.total().astype(BF16)
    key_z.start()
    value_mid[...] = value_z.total().astype(BF16)
    value_y.start()
    for step in range(1, 4):
        key_z.step(step)
        value_y.step(step)
    key_sum = key_z.total()
    value_sum = value_y.total()

    parts = []
    for h in range(2):
        cols = slice(h * HD, (h + 1) * HD)
        rows = raw[:, cols]
        inverse = lax.rsqrt(jnp.mean(rows * rows, axis=1, keepdims=True) + EPS)
        up = key_sum[:, cols] * key_gain[...]
        row_inner = jnp.mean(up * rows, axis=1, keepdims=True)
        parts.append((inverse * (up - rows * (inverse * inverse * row_inner))).astype(BF16))
    raw_grad = jnp.concatenate(parts, axis=1)
    value_grad = value_sum.astype(BF16)

    lat = latents_t[...]
    for c, grad in enumerate((raw_grad, value_grad)):
        share = jnp.dot(lat, grad, preferred_element_type=F32).astype(BF16)
        weights[:, :, :, c * COLS:(c + 1) * COLS] = share.reshape(NZ, NL, PAD, COLS)
    weight_z = ReduceRing(
        lambda b, half: halves(weights.at[b], NL // 2, half), inbox(weights_in, NL // 2),
        me.z, me.at_z(1), me.at_z(-1), ring_send, ring_recv, 32)
    weight_z.start()

    wide[...] = dot(raw_grad, key_weight[...], 1, 1) + dot(value_grad, value_weight[...], 1, 1)
    spread[...] = jnp.zeros_like(spread)
    for d in range(2 * NX):
        for n in range(VD // HD):
            spread[d, 4 * n:4 * n + 4, :] = wide[4 * d:4 * d + 4, n * HD:(n + 1) * HD]
    shares[...] = spread[...].astype(BF16)
    head_copies = []
    for d in range(1, 2 * NX):
        copy = remote(
            shares.at[lax.rem(me.head + d, 2 * NX)], shares_in.at[d], head_send, head_recv, d, me.at_head(d))
        copy.start()
        head_copies.append(copy)

    for step in range(1, 4):
        weight_z.step(step)
    low_out[...] = weight_z.total().astype(BF16)
    low_copies = []
    for d in range(1, NL):
        copy = remote(low_out.at[lax.rem(me.yl + d, NL)], low_in.at[d], low_send, low_recv, d, me.at_low(d))
        copy.start()
        low_copies.append(copy)

    total = shares[me.head].astype(F32)
    for d in range(1, 2 * NX):
        place = shares_in.at[d]
        remote(place, place, head_send, head_recv, d, me.at_head(d)).wait_recv()
        total = total + place[...].astype(F32)
    spread[0] = total
    for n in range(VD // HD):
        wide[0:4, n * HD:(n + 1) * HD] = spread[0, 4 * n:4 * n + 4, :]
    out_latents[...] = wide[0:4, :].astype(BF16)

    total = low_out[me.yl].astype(F32)
    for d in range(1, NL):
        place = low_in.at[d]
        remote(place, place, low_send, low_recv, d, me.at_low(d)).wait_recv()
        total = total + place[...].astype(F32)
    out_key_weight[...] = total[0:40, 0:COLS]
    out_value_weight[...] = total[0:40, COLS:]

    for d in range(1, NX):
        source = lax.rem(me.xc + (NX - d), NX)
        for c in range(2):
            place = out_queries.at[:, cols_of(c, source)]
            remote(place, place, swap_send, swap_recv, (d - 1) * 2 + c, me.at_x(d)).wait_recv()
    for copy in own:
        copy.wait()
    for copy in swaps + head_copies + low_copies:
        copy.wait_send()
    for ring in (key_y, value_z, key_z, value_y, weight_z):
        ring.finish()


VMEM = pl.BlockSpec(memory_space=pltpu.VMEM)
SMEM = pl.BlockSpec(memory_space=pltpu.SMEM)
HBM = pl.BlockSpec(memory_space=pl.ANY)
LIMIT = 48 * 1024 * 1024
DMA = pltpu.SemaphoreType.DMA


def struct(shape, dtype):
    return jax.ShapeDtypeStruct(shape, dtype)


def body(
    queries,
    out_grad,
    latents,
    key_weight,
    value_weight,
    query_gain,
    key_gain,
    gate_alpha,
    media_slot,
    media_position,
    tile_list,
):
    seq = lax.axis_index("seq")
    high = lax.div(lax.axis_index("head"), NX)
    flat = latents.reshape(LAT, VD)
    gain_q = query_gain.reshape(1, HD)
    gain_k = key_gain.reshape(1, HD)

    q_rows, g_rows, keys, values, raw = pl.pallas_call(
        gather_kernel,
        out_shape=(
            struct((2, TOK, COLS), BF16),
            struct((2, TOK, COLS), BF16),
            struct((NY, NZ, LAT, COLS), BF16),
            struct((NZ, NY, LAT, COLS), BF16),
            struct((LAT, COLS), F32),
        ),
        in_specs=[HBM, HBM, VMEM, VMEM, VMEM, VMEM],
        out_specs=(HBM, HBM, VMEM, VMEM, VMEM),
        scratch_shapes=[DMA((32,)), DMA((32,)), DMA((28,)), DMA((28,)), DMA((4,))],
        compiler_params=pltpu.CompilerParams(collective_id=0, has_side_effects=True, vmem_limit_bytes=LIMIT),
        name="gather",
    )(queries, out_grad, flat, key_weight, value_weight, gain_k)

    lists = lax.dynamic_slice_in_dim(tile_list, high * 2, 2, 0)
    image_range = jnp.arange(SLOTS, dtype=jnp.int32)
    live = lists >= 0
    matches = lists[:, :, None] == image_range
    slot = jnp.sum(jnp.where(matches, media_slot, 0), axis=2)
    place = jnp.where(live, jnp.sum(jnp.where(matches, media_position, 0), axis=2), DEAD)
    entry_value = lax.rem(slot, NZ) * NY + lax.div(slot, NZ)
    hit = live[:, :, None] & (slot[:, :, None] == image_range)
    entry_range = jnp.arange(LIST, dtype=jnp.int32)[None, :, None]
    slot_entry = LIST - jnp.sum(jnp.where(hit, LIST - entry_range, 0), axis=1)
    first_token = (seq * (2 * TOK) + high * TOK).reshape(1).astype(jnp.int32)

    grad_q, grad_keys, grad_values = pl.pallas_call(
        attend_kernel,
        out_shape=(
            struct((2, TOK, COLS), BF16),
            struct((NY, NZ, LAT, COLS), BF16),
            struct((NZ, NY, LAT, COLS), BF16),
        ),
        in_specs=[SMEM] * 6 + [VMEM] * 5,
        out_specs=(VMEM, VMEM, VMEM),
        scratch_shapes=[
            pltpu.VMEM((LIST * LAT, COLS), BF16),
            pltpu.VMEM((LIST * LAT, COLS), BF16),
            pltpu.VMEM((2, 2, LIST + 1, LAT, COLS), F32),
            pltpu.VMEM((2, 2, LIST + 1, LAT, COLS), F32),
        ],
        compiler_params=pltpu.CompilerParams(vmem_limit_bytes=LIMIT),
        name="attend",
    )(
        slot, entry_value, place, slot_entry, first_token, jnp.tanh(gate_alpha),
        q_rows, g_rows, keys.reshape(2 * SLOTS, LAT, COLS), values.reshape(2 * SLOTS, LAT, COLS), gain_q,
    )

    latents_t = flat.T.reshape(NL, NZ, VD // SLOTS, LAT).transpose(1, 0, 2, 3)
    latents_t = jnp.pad(latents_t, ((0, 0), (0, 0), (0, PAD - VD // SLOTS), (0, 0)))
    latents_t = latents_t.reshape(NZ * NL * PAD, LAT)

    block = (LAT, COLS)
    return pl.pallas_call(
        reduce_kernel,
        out_shape=(
            struct((OWN, 2 * NX * COLS), BF16),
            struct((4, VD), BF16),
            struct((VD // SLOTS, COLS), F32),
            struct((VD // SLOTS, COLS), F32),
        ),
        in_specs=[HBM, HBM, HBM] + [VMEM] * 5,
        out_specs=(HBM, VMEM, VMEM, VMEM),
        scratch_shapes=[
            pltpu.VMEM((NY, NZ) + block, BF16),
            pltpu.VMEM((NZ, NY) + block, BF16),
            pltpu.VMEM((2, 4, NZ) + block, BF16),
            pltpu.VMEM((2, 4, NY) + block, BF16),
            pltpu.VMEM((NZ,) + block, BF16),
            pltpu.VMEM((NY,) + block, BF16),
            pltpu.VMEM((2, 4) + block, BF16),
            pltpu.VMEM((2, 4) + block, BF16),
            pltpu.VMEM((2 * NX, PAD, HD), BF16),
            pltpu.VMEM((2 * NX, PAD, HD), BF16),
            pltpu.VMEM((2 * NX, PAD, HD), F32),
            pltpu.VMEM((LAT, VD), F32),
            pltpu.VMEM((NZ, NL, PAD, 2 * COLS), BF16),
            pltpu.VMEM((2, 4, NL, PAD, 2 * COLS), BF16),
            pltpu.VMEM((NL, PAD, 2 * COLS), BF16),
            pltpu.VMEM((NL, PAD, 2 * COLS), BF16),
            DMA((2,)),
            DMA((40,)), DMA((40,)), DMA((14,)), DMA((14,)), DMA((2,)),
            DMA((16,)), DMA((16,)), DMA((4,)), DMA((4,)),
        ],
        compiler_params=pltpu.CompilerParams(collective_id=1, has_side_effects=True, vmem_limit_bytes=LIMIT),
        name="reduce",
    )(grad_q, grad_keys, grad_values, raw, gain_k, key_weight, value_weight, latents_t)


def solution(mesh):
    in_specs = (
        P(("seq", "head"), None),
        P(("seq", "head"), None),
        P("seq", None, None),
        P(None, "head"),
        P(None, "head"),
        P(),
        P(),
        P(),
        P(),
        P(),
        P("seq", None),
    )
    out_specs = (
        P(("seq", "head"), None),
        P("seq", "head", None),
        P("seq", "head"),
        P("seq", "head"),
    )

    def run(*args):
        query_grad, latent_grad, key_weight_grad, value_weight_grad = body(*args)
        return (query_grad, latent_grad.reshape(1, 4, VD), key_weight_grad, value_weight_grad)

    return jax.shard_map(run, mesh=mesh, in_specs=in_specs, out_specs=out_specs, check_vma=False)
```

```python
import jax
import jax.numpy as jnp
from jax import lax
from jax.experimental import pallas as pl
from jax.experimental.pallas import tpu as pltpu
from jax.sharding import PartitionSpec as P

HD = 128
EPS = 1e-06
SCALE = HD ** (-0.5)
LOG2E = 1.4426950408889634
MESH = pl.DeviceIdType.MESH

NZ = 8
NL = 4
NY = 8
NX = 8
LAT = 64
LIST = 8
TILE = 512
TOK = 1024
OWN = 128
COLS = 256
VD = 1280
PAD = 48
SLOTS = 32
DEAD = 1 << 30

F32 = jnp.float32
BF16 = jnp.bfloat16


def dot(a, b, ca, cb):
    return lax.dot_general(a, b, (((ca,), (cb,)), ((), ())), preferred_element_type=F32)


class Place:
    def __init__(self):
        self.seq = lax.axis_index("seq")
        self.head = lax.axis_index("head")
        self.z = lax.rem(self.seq, NZ)
        self.yl = lax.div(self.seq, NZ)
        self.yh = lax.div(self.head, NX)
        self.xc = lax.rem(self.head, NX)
        self.y = self.yh * NL + self.yl

    def at_y(self, step):
        y = lax.rem(self.y + (step + NY), NY)
        return (lax.rem(y, NL) * NZ + self.z, lax.div(y, NL) * NX + self.xc)

    def at_z(self, step):
        z = lax.rem(self.z + (step + NZ), NZ)
        return (self.yl * NZ + z, self.head)

    def at_x(self, step):
        return (self.seq, self.yh * NX + lax.rem(self.xc + step, NX))

    def at_head(self, step):
        return (self.seq, lax.rem(self.head + step, 2 * NX))

    def at_low(self, step):
        return (lax.rem(self.yl + step, NL) * NZ + self.z, self.head)


def greet(partners):
    barrier = pltpu.get_barrier_semaphore()
    for partner in partners:
        pl.semaphore_signal(barrier, inc=1, device_id=partner, device_id_type=MESH)
    pl.semaphore_wait(barrier, len(partners))


def remote(src, dst, sends, recvs, sem, device):
    return pltpu.make_async_remote_copy(
        src_ref=src,
        dst_ref=dst,
        send_sem=sends.at[sem],
        recv_sem=recvs.at[sem],
        device_id=device,
        device_id_type=MESH,
    )


class GatherRing:
    def __init__(self, block, me, right, left, sends, recvs, base):
        self.block, self.me, self.targets = block, me, (right, left)
        self.sends, self.recvs, self.base = sends, recvs, base
        self.started = []

    def copy(self, way, step, shift):
        offset = (-step - shift) if way == 0 else (step + shift)
        ref = self.block(lax.rem(self.me + (offset + 8), 8), way if step == 3 else None)
        return remote(ref, ref, self.sends, self.recvs, self.base + way * 4 + step, self.targets[way])

    def start(self, step):
        for way in (0, 1):
            copy = self.copy(way, step, 0)
            copy.start()
            self.started.append(copy)

    def wait(self, step):
        for way in (0, 1):
            self.copy(way, step, 1).wait_recv()

    def finish(self):
        for copy in self.started:
            copy.wait_send()


class ReduceRing:
    def __init__(self, own, inbox, me, right, left, sends, recvs, base):
        self.own, self.inbox, self.me, self.targets = own, inbox, me, (right, left)
        self.sends, self.recvs, self.base = sends, recvs, base
        self.started = []

    def index(self, way, step):
        offset = 4 - step if way == 0 else step + 4
        return lax.rem(self.me + offset, 8)

    def send(self, way, step, src):
        copy = remote(
            src, self.inbox(way, step), self.sends, self.recvs, self.base + way * 4 + step, self.targets[way]
        )
        copy.start()
        self.started.append(copy)

    def arrive(self, way, step):
        ref = self.inbox(way, step)
        remote(ref, ref, self.sends, self.recvs, self.base + way * 4 + step, self.targets[way]).wait_recv()

    def start(self):
        for way in (0, 1):
            self.send(way, 0, self.own(self.index(way, 0), way))

    def step(self, step):
        for way in (0, 1):
            self.arrive(way, step - 1)
            index = self.index(way, step)
            here = self.inbox(way, step - 1)
            if step == 1:
                part = self.own(index, way)
                part[...] = (part[...].astype(F32) + here[...].astype(F32)).astype(BF16)
                self.send(way, 1, self.own(index, None))
            else:
                here[...] = (here[...].astype(F32) + self.own(index, None)[...].astype(F32)).astype(BF16)
                self.send(way, step, here)

    def total(self):
        for way in (0, 1):
            self.arrive(way, 3)
        return (
            self.own(self.me, None)[...].astype(F32)
            + self.inbox(0, 3)[...].astype(F32)
            + self.inbox(1, 3)[...].astype(F32)
        )

    def finish(self):
        for copy in self.started:
            copy.wait_send()


def halves(ref, size, half):
    return ref if half is None else ref.at[pl.ds(half * size, size)]


def scratch(*shape, dtype=BF16):
    return pltpu.VMEM(shape, dtype)


PIECE = dict(
    keys=scratch(NY, NZ, LAT, HD),
    values=scratch(NZ, NY, LAT, HD),
    q_rows=scratch(2, TOK, HD),
    g_rows=scratch(2, TOK, HD),
    grad_q=scratch(2, TOK, HD),
    grad_keys=scratch(NY, NZ, LAT, HD),
    grad_values=scratch(NZ, NY, LAT, HD),
    key_in=scratch(2, 4, NZ, LAT, HD),
    value_in=scratch(2, 4, NY, LAT, HD),
    key_mid=scratch(NZ, LAT, HD),
    value_mid=scratch(NY, LAT, HD),
    key_low=scratch(2, 4, LAT, HD),
    value_low=scratch(2, 4, LAT, HD),
    weights=scratch(NZ, NL, PAD, 2 * HD),
    weights_in=scratch(2, 4, NL, PAD, 2 * HD),
    low_out=scratch(NL, PAD, 2 * HD),
    low_in=scratch(NL, PAD, 2 * HD),
    ring_send=pltpu.SemaphoreType.DMA((72,)),
    ring_recv=pltpu.SemaphoreType.DMA((72,)),
    swap_send=pltpu.SemaphoreType.DMA((28,)),
    swap_recv=pltpu.SemaphoreType.DMA((28,)),
    swap_own=pltpu.SemaphoreType.DMA((4,)),
    back_send=pltpu.SemaphoreType.DMA((14,)),
    back_recv=pltpu.SemaphoreType.DMA((14,)),
    back_own=pltpu.SemaphoreType.DMA((2,)),
    low_send=pltpu.SemaphoreType.DMA((4,)),
    low_recv=pltpu.SemaphoreType.DMA((4,)),
)
SHARED = dict(
    latents=scratch(LAT, VD),
    key_weight=scratch(VD, COLS),
    value_weight=scratch(VD, COLS),
    raw=scratch(LAT, COLS, dtype=F32),
    key_tile=scratch(LIST * LAT, HD),
    value_tile=scratch(LIST * LAT, HD),
    key_sums=scratch(2, 2, LIST + 1, LAT, HD, dtype=F32),
    value_sums=scratch(2, 2, LIST + 1, LAT, HD, dtype=F32),
    shares=scratch(2 * NX, PAD, HD),
    shares_in=scratch(2 * NX, PAD, HD),
    spread=scratch(2 * NX, PAD, HD, dtype=F32),
    wide=scratch(LAT, VD, dtype=F32),
    load_sem=pltpu.SemaphoreType.DMA((3,)),
    head_send=pltpu.SemaphoreType.DMA((16,)),
    head_recv=pltpu.SemaphoreType.DMA((16,)),
)


class Refs:
    def __init__(self, names, refs):
        self.__dict__.update(zip(names, refs))


def inbox(buffer, size):
    def place(way, step):
        ref = buffer.at[way, step]
        return ref.at[pl.ds(way * size, size)] if step == 0 else ref

    return place


def gather_rings(me, p):
    y, z = (me.at_y(1), me.at_y(-1)), (me.at_z(1), me.at_z(-1))
    sems = (p.ring_send, p.ring_recv)
    first = (
        GatherRing(lambda b, half: halves(p.keys.at[me.y, b], LAT // 2, half), me.z, *z, *sems, 0),
        GatherRing(lambda b, half: halves(p.values.at[me.z, b], LAT // 2, half), me.y, *y, *sems, 8),
    )
    second = (
        GatherRing(lambda b, half: halves(p.keys.at[b], NZ // 2, half), me.y, *y, *sems, 16),
        GatherRing(lambda b, half: halves(p.values.at[b], NY // 2, half), me.z, *z, *sems, 24),
    )
    return first, second


def reduce_rings(me, p):
    y, z = (me.at_y(1), me.at_y(-1)), (me.at_z(1), me.at_z(-1))
    sems = (p.ring_send, p.ring_recv)
    key_y = ReduceRing(
        lambda b, half: halves(p.grad_keys.at[b], NZ // 2, half), inbox(p.key_in, NZ // 2), me.y, *y, *sems, 32)
    value_z = ReduceRing(
        lambda b, half: halves(p.grad_values.at[b], NY // 2, half), inbox(p.value_in, NY // 2), me.z, *z, *sems, 40)
    key_z = ReduceRing(
        lambda b, half: halves(p.key_mid.at[b], LAT // 2, half), inbox(p.key_low, LAT // 2), me.z, *z, *sems, 48)
    value_y = ReduceRing(
        lambda b, half: halves(p.value_mid.at[b], LAT // 2, half), inbox(p.value_low, LAT // 2), me.y, *y, *sems, 56)
    weight_z = ReduceRing(
        lambda b, half: halves(p.weights.at[b], NL // 2, half), inbox(p.weights_in, NL // 2), me.z, *z, *sems, 64)
    return key_y, value_z, key_z, value_y, weight_z


def columns(c, place, h):
    return pl.ds(pl.multiple_of((c * NX + place) * COLS + h * HD, HD), HD)


def rows_of(place):
    return pl.ds(pl.multiple_of(place * OWN, OWN), OWN)


class Swap:
    def __init__(self, me, p, h, queries, out_grad):
        self.me, self.p = me, p
        self.sent, self.own = [], []
        for d in range(NX):
            to = lax.rem(me.xc + d, NX)
            for n, (src, dst) in enumerate(((queries, p.q_rows), (out_grad, p.g_rows))):
                for c in range(2):
                    src_ref = src.at[:, columns(c, to, h)]
                    dst_ref = dst.at[c, rows_of(me.xc)]
                    if d == 0:
                        copy = pltpu.make_async_copy(src_ref, dst_ref, p.swap_own.at[n * 2 + c])
                        self.own.append(copy)
                    else:
                        sem = (d - 1) * 4 + n * 2 + c
                        copy = remote(src_ref, dst_ref, p.swap_send, p.swap_recv, sem, me.at_x(d))
                        self.sent.append(copy)
                    copy.start()

    def wait(self):
        me, p = self.me, self.p
        for d in range(1, NX):
            source = lax.rem(me.xc + (NX - d), NX)
            for n, dst in enumerate((p.q_rows, p.g_rows)):
                for c in range(2):
                    ref = dst.at[c, rows_of(source)]
                    sem = (d - 1) * 4 + n * 2 + c
                    remote(ref, ref, p.swap_send, p.swap_recv, sem, me.at_x(d)).wait_recv()
        for copy in self.own:
            copy.wait()

    def finish(self):
        for copy in self.sent:
            copy.wait_send()


class SwapBack:
    def __init__(self, me, p, h, out):
        self.me, self.p, self.h, self.out = me, p, h, out
        self.sent, self.own = [], []
        for d in range(NX):
            to = lax.rem(me.xc + d, NX)
            for c in range(2):
                src_ref = p.grad_q.at[c, rows_of(to)]
                dst_ref = out.at[:, columns(c, me.xc, h)]
                if d == 0:
                    copy = pltpu.make_async_copy(src_ref, dst_ref, p.back_own.at[c])
                    self.own.append(copy)
                else:
                    copy = remote(src_ref, dst_ref, p.back_send, p.back_recv, (d - 1) * 2 + c, me.at_x(d))
                    self.sent.append(copy)
                copy.start()

    def finish(self):
        me, p = self.me, self.p
        for d in range(1, NX):
            source = lax.rem(me.xc + (NX - d), NX)
            for c in range(2):
                ref = self.out.at[:, columns(c, source, self.h)]
                remote(ref, ref, p.back_send, p.back_recv, (d - 1) * 2 + c, me.at_x(d)).wait_recv()
        for copy in self.own:
            copy.wait()
        for copy in self.sent:
            copy.wait_send()


def attend(me, p, s, t, c, entries, gate, gain):
    for e in range(LIST):
        rows = slice(e * LAT, (e + 1) * LAT)
        slot = entries[t][e][0]
        s.key_tile[rows, :] = p.keys[c * NL + lax.div(slot, NZ), lax.rem(slot, NZ)]
        s.value_tile[rows, :] = p.values[lax.rem(slot, NZ), c * NL + lax.div(slot, NZ)]
    kt = s.key_tile[...]
    vt = s.value_tile[...]
    base = t * TILE
    q = p.q_rows[c, base:base + TILE, :].astype(F32)
    g = p.g_rows[c, base:base + TILE, :].astype(F32)
    inverse = lax.rsqrt(jnp.mean(q * q, axis=1, keepdims=True) + EPS)
    q_hat = (q * inverse * gain).astype(BF16)
    ctx = (gate * g).astype(BF16)
    scores = dot(kt, q_hat, 1, 1)
    grad_probs = dot(vt, ctx, 1, 1)
    token = me.seq * (2 * TOK) + me.yh * TOK + base + lax.broadcasted_iota(jnp.int32, (1, TILE), 1)
    total = jnp.zeros((1, TILE), F32)
    inner = jnp.zeros((1, TILE), F32)
    dead = jnp.ones((1, TILE), F32)
    exps = []
    for e in range(LIST):
        rows = slice(e * LAT, (e + 1) * LAT)
        live = entries[t][e][1] < token
        dead = jnp.where(live, 0.0, dead)
        x = jnp.where(live, jnp.exp2(scores[rows] * (SCALE * LOG2E)), 0.0)
        exps.append(x)
        total = total + jnp.sum(x, axis=0, keepdims=True)
        inner = inner + jnp.sum(x * grad_probs[rows], axis=0, keepdims=True)
    norm = 1.0 / (total + dead)
    inner = inner * norm
    probs = []
    grads = []
    for e in range(LIST):
        rows = slice(e * LAT, (e + 1) * LAT)
        prob = exps[e] * norm
        probs.append(prob.astype(BF16))
        grads.append((prob * (grad_probs[rows] - inner)).astype(BF16))
    probs = jnp.concatenate(probs, axis=0)
    grads = jnp.concatenate(grads, axis=0)
    s.key_sums[t, c, 0:LIST] = (dot(grads, q_hat, 1, 0) * SCALE).reshape(LIST, LAT, HD)
    s.value_sums[t, c, 0:LIST] = dot(probs, ctx, 1, 0).reshape(LIST, LAT, HD)
    up = dot(kt.T, grads, 1, 0).T * SCALE * gain
    row_inner = jnp.mean(up * q, axis=1, keepdims=True)
    p.grad_q[c, base:base + TILE, :] = (inverse * (up - q * (inverse * inverse * row_inner))).astype(BF16)


def to_slots(p, s, entries):
    def one_slot(slot, carry):
        z = lax.rem(slot, NZ)
        low = lax.div(slot, NZ)
        place = []
        for t in range(2):
            found = jnp.int32(LIST)
            for e in range(LIST):
                found = jnp.where(entries[t][e][2] == slot, e, found)
            place.append(found)
        for c in range(2):
            p.grad_keys[c * NL + low, z] = (
                s.key_sums[0, c, place[0]] + s.key_sums[1, c, place[1]]).astype(BF16)
            p.grad_values[z, c * NL + low] = (
                s.value_sums[0, c, place[0]] + s.value_sums[1, c, place[1]]).astype(BF16)
        return carry

    lax.fori_loop(0, SLOTS, one_slot, 0)


def kernel(
    tile_list, media_slot, media_position, gate_alpha,
    queries, out_grad, latents, key_weight, value_weight, query_gain, key_gain,
    out_queries, out_latents, out_key_weight, out_value_weight,
    *refs,
):
    count = len(PIECE)
    pieces = [Refs(PIECE, refs[h * count:(h + 1) * count]) for h in range(2)]
    s = Refs(SHARED, refs[2 * count:])
    me = Place()
    loads = [
        pltpu.make_async_copy(src, dst, s.load_sem.at[n])
        for n, (src, dst) in enumerate(
            ((latents, s.latents), (key_weight, s.key_weight), (value_weight, s.value_weight)))
    ]
    for load in loads:
        load.start()
    greet(
        [me.at_y(1), me.at_y(-1), me.at_z(1), me.at_z(-1)]
        + [me.at_head(d) for d in range(1, 2 * NX)]
        + [me.at_x(d) for d in range(1, NX)]
        + [me.at_low(d) for d in range(1, NL)]
    )
    for load in loads:
        load.wait()

    gain_k = key_gain[...]
    flat = s.latents[...]
    s.raw[...] = jnp.dot(flat, s.key_weight[...], preferred_element_type=F32)
    own_values = jnp.dot(flat, s.value_weight[...], preferred_element_type=F32).astype(BF16)
    for h, p in enumerate(pieces):
        cols = slice(h * HD, (h + 1) * HD)
        part = s.raw[:, cols]
        inverse = lax.rsqrt(jnp.mean(part * part, axis=1, keepdims=True) + EPS)
        p.keys[me.y, me.z] = (part * inverse * gain_k).astype(BF16)
        p.values[me.z, me.y] = own_values[:, cols]

    firsts, seconds = zip(*[gather_rings(me, p) for p in pieces])

    def start(rings, step):
        for ring in rings:
            ring.start(step)

    def follow(rings, step):
        for ring in rings:
            ring.wait(step)
            if step < 3:
                ring.start(step + 1)

    start(firsts[0], 0)
    start(firsts[1], 0)
    swaps = [Swap(me, p, h, queries, out_grad) for h, p in enumerate(pieces)]

    entries = []
    for t in range(2):
        entries.append([])
        for e in range(LIST):
            image = tile_list[me.yh * 2 + t, e]
            held = jnp.maximum(image, 0)
            slot = media_slot[held]
            entries[t].append((
                slot,
                jnp.where(image >= 0, media_position[held], DEAD),
                jnp.where(image >= 0, slot, SLOTS),
            ))
    gate = jnp.tanh(jnp.full((1, HD), gate_alpha[0], F32))
    gain_q = query_gain[...]
    for t in range(2):
        for c in range(2):
            s.key_sums[t, c, LIST] = jnp.zeros((LAT, HD), F32)
            s.value_sums[t, c, LIST] = jnp.zeros((LAT, HD), F32)

    for step in range(4):
        follow(firsts[0], step)
        follow(firsts[1], step)
    start(seconds[0], 0)
    follow(seconds[0], 0)
    follow(seconds[0], 1)
    start(seconds[1], 0)
    follow(seconds[0], 2)
    follow(seconds[1], 0)
    follow(seconds[0], 3)
    follow(seconds[1], 1)

    units = [(t, c) for t in range(2) for c in range(2)]

    def run(h, n):
        t, c = units[n]
        attend(me, pieces[h], s, t, c, entries, gate, gain_q)

    swaps[0].wait()
    run(0, 0)
    run(0, 1)
    follow(seconds[1], 2)
    run(0, 2)
    run(0, 3)
    to_slots(pieces[0], s, entries)
    sums = [reduce_rings(me, p) for p in pieces]
    raw_grads, value_grads, low_copies, head_copies = {}, {}, [], []

    def tasks(h):
        p = pieces[h]
        key_y, value_z, key_z, value_y, weight_z = sums[h]

        def begin():
            key_y.start()
            value_z.start()

        def first(step):
            def act():
                key_y.step(step)
                value_z.step(step)
            return act

        def turn():
            p.key_mid[...] = key_y.total().astype(BF16)
            key_z.start()
            p.value_mid[...] = value_z.total().astype(BF16)
            value_y.start()

        def second(step):
            def act():
                key_z.step(step)
                value_y.step(step)
            return act

        def own_image():
            key_sum = key_z.total()
            value_sum = value_y.total()
            part = s.raw[:, h * HD:(h + 1) * HD]
            inverse = lax.rsqrt(jnp.mean(part * part, axis=1, keepdims=True) + EPS)
            up = key_sum * gain_k
            row_inner = jnp.mean(up * part, axis=1, keepdims=True)
            raw_grads[h] = (inverse * (up - part * (inverse * inverse * row_inner))).astype(BF16)
            value_grads[h] = value_sum.astype(BF16)
            both = jnp.concatenate([raw_grads[h], value_grads[h]], axis=1)
            share = dot(s.latents[...], both, 0, 0)
            for n in range(SLOTS):
                block = share[n * 40:(n + 1) * 40]
                block = jnp.concatenate([block, jnp.zeros((PAD - 40, 2 * HD), F32)], axis=0)
                p.weights[n % NZ, n // NZ] = block.astype(BF16)
            weight_z.start()
            if h == 1:
                latent_share()

        def third(step):
            def act():
                weight_z.step(step)
            return act

        def low():
            p.low_out[...] = weight_z.total().astype(BF16)
            for d in range(1, NL):
                copy = remote(
                    p.low_out.at[lax.rem(me.yl + d, NL)], p.low_in.at[d], p.low_send, p.low_recv, d, me.at_low(d))
                copy.start()
                low_copies.append(copy)

        def last():
            total = p.low_out[me.yl].astype(F32)
            for d in range(1, NL):
                ref = p.low_in.at[d]
                remote(ref, ref, p.low_send, p.low_recv, d, me.at_low(d)).wait_recv()
                total = total + ref[...].astype(F32)
            cols = slice(h * HD, (h + 1) * HD)
            out_key_weight[:, cols] = total[0:40, 0:HD]
            out_value_weight[:, cols] = total[0:40, HD:]

        return (
            [begin] + [first(step) for step in (1, 2, 3)] + [turn] + [second(step) for step in (1, 2, 3)]
            + [own_image] + [third(step) for step in (1, 2, 3)] + [low, last]
        )

    def latent_share():
        raw_grad = jnp.concatenate([raw_grads[0], raw_grads[1]], axis=1)
        value_grad = jnp.concatenate([value_grads[0], value_grads[1]], axis=1)
        s.wide[...] = dot(raw_grad, s.key_weight[...], 1, 1) + dot(value_grad, s.value_weight[...], 1, 1)
        s.spread[...] = jnp.zeros_like(s.spread)
        for d in range(2 * NX):
            for n in range(VD // HD):
                s.spread[d, 4 * n:4 * n + 4, :] = s.wide[4 * d:4 * d + 4, n * HD:(n + 1) * HD]
        s.shares[...] = s.spread[...].astype(BF16)
        for d in range(1, 2 * NX):
            copy = remote(
                s.shares.at[lax.rem(me.head + d, 2 * NX)], s.shares_in.at[d], s.head_send, s.head_recv, d,
                me.at_head(d))
            copy.start()
            head_copies.append(copy)

    left = [tasks(0), tasks(1)]

    def go(h):
        left[h].pop(0)()

    go(0)
    backs = [SwapBack(me, pieces[0], 0, out_queries)]
    follow(seconds[1], 3)
    swaps[1].wait()
    run(1, 0)
    run(1, 1)
    go(0)
    run(1, 2)
    run(1, 3)
    to_slots(pieces[1], s, entries)
    go(1)
    go(0)
    backs.append(SwapBack(me, pieces[1], 1, out_queries))
    while left[1]:
        go(1)
        if left[0]:
            go(0)

    total = s.shares[me.head].astype(F32)
    for d in range(1, 2 * NX):
        ref = s.shares_in.at[d]
        remote(ref, ref, s.head_send, s.head_recv, d, me.at_head(d)).wait_recv()
        total = total + ref[...].astype(F32)
    s.spread[0] = total
    for n in range(VD // HD):
        s.wide[0:4, n * HD:(n + 1) * HD] = s.spread[0, 4 * n:4 * n + 4, :]
    out_latents[...] = s.wide[0:4, :].astype(BF16)

    for swap in swaps + backs:
        swap.finish()
    for copy in head_copies + low_copies:
        copy.wait_send()
    for rings in firsts + seconds + tuple(sums):
        for ring in rings:
            ring.finish()


VMEM = pl.BlockSpec(memory_space=pltpu.VMEM)
SMEM = pl.BlockSpec(memory_space=pltpu.SMEM)
HBM = pl.BlockSpec(memory_space=pl.ANY)
LIMIT = 60 * 1024 * 1024


def struct(shape, dtype):
    return jax.ShapeDtypeStruct(shape, dtype)


def body(
    queries,
    out_grad,
    latents,
    key_weight,
    value_weight,
    query_gain,
    key_gain,
    gate_alpha,
    media_slot,
    media_position,
    tile_list,
):
    query_grad, latent_grad, key_weight_grad, value_weight_grad = pl.pallas_call(
        kernel,
        out_shape=(
            struct((OWN, 2 * NX * COLS), BF16),
            struct((4, VD), BF16),
            struct((VD // SLOTS, COLS), F32),
            struct((VD // SLOTS, COLS), F32),
        ),
        in_specs=[SMEM] * 4 + [HBM] * 5 + [VMEM] * 2,
        out_specs=(HBM, VMEM, VMEM, VMEM),
        scratch_shapes=list(PIECE.values()) * 2 + list(SHARED.values()),
        compiler_params=pltpu.CompilerParams(collective_id=0, has_side_effects=True, vmem_limit_bytes=LIMIT),
        name="backward",
    )(
        tile_list, media_slot, media_position, gate_alpha,
        queries, out_grad, latents.reshape(LAT, VD), key_weight, value_weight,
        query_gain.reshape(1, HD), key_gain.reshape(1, HD),
    )
    return (query_grad, latent_grad.reshape(1, 4, VD), key_weight_grad, value_weight_grad)


def solution(mesh):
    in_specs = (
        P(("seq", "head"), None),
        P(("seq", "head"), None),
        P("seq", None, None),
        P(None, "head"),
        P(None, "head"),
        P(),
        P(),
        P(),
        P(),
        P(),
        P("seq", None),
    )
    out_specs = (
        P(("seq", "head"), None),
        P("seq", "head", None),
        P("seq", "head"),
        P("seq", "head"),
    )
    return jax.shard_map(body, mesh=mesh, in_specs=in_specs, out_specs=out_specs, check_vma=False)
```

```python
import jax
import jax.numpy as jnp
from jax import lax
from jax.experimental import pallas as pl
from jax.experimental.pallas import tpu as pltpu
from jax.sharding import PartitionSpec as P

HD = 128
EPS = 1e-06
SCALE = HD ** (-0.5)
LOG2E = 1.4426950408889634
MESH = pl.DeviceIdType.MESH

NZ = 8
NL = 4
NY = 8
NX = 8
LAT = 64
LIST = 8
TILE = 512
TOK = 1024
OWN = 128
COLS = 256
VD = 1280
PAD = 48
SLOTS = 32
DEAD = 1 << 30

F32 = jnp.float32
BF16 = jnp.bfloat16


def dot(a, b, ca, cb):
    return lax.dot_general(a, b, (((ca,), (cb,)), ((), ())), preferred_element_type=F32)


class Place:
    def __init__(self):
        self.seq = lax.axis_index("seq")
        self.head = lax.axis_index("head")
        self.z = lax.rem(self.seq, NZ)
        self.yl = lax.div(self.seq, NZ)
        self.yh = lax.div(self.head, NX)
        self.xc = lax.rem(self.head, NX)
        self.y = self.yh * NL + self.yl

    def at_y(self, step):
        y = lax.rem(self.y + (step + NY), NY)
        return (lax.rem(y, NL) * NZ + self.z, lax.div(y, NL) * NX + self.xc)

    def at_z(self, step):
        z = lax.rem(self.z + (step + NZ), NZ)
        return (self.yl * NZ + z, self.head)

    def at_x(self, step):
        return (self.seq, self.yh * NX + lax.rem(self.xc + step, NX))

    def at_head(self, step):
        return (self.seq, lax.rem(self.head + step, 2 * NX))

    def at_low(self, step):
        return (lax.rem(self.yl + step, NL) * NZ + self.z, self.head)


def greet(partners):
    barrier = pltpu.get_barrier_semaphore()
    for partner in partners:
        pl.semaphore_signal(barrier, inc=1, device_id=partner, device_id_type=MESH)
    pl.semaphore_wait(barrier, len(partners))


def remote(src, dst, sends, recvs, sem, device):
    return pltpu.make_async_remote_copy(
        src_ref=src,
        dst_ref=dst,
        send_sem=sends.at[sem],
        recv_sem=recvs.at[sem],
        device_id=device,
        device_id_type=MESH,
    )


class GatherRing:
    def __init__(self, block, me, right, left, sends, recvs, base):
        self.block, self.me, self.targets = block, me, (right, left)
        self.sends, self.recvs, self.base = sends, recvs, base
        self.started = []

    def copy(self, way, step, shift):
        offset = (-step - shift) if way == 0 else (step + shift)
        ref = self.block(lax.rem(self.me + (offset + 8), 8), way if step == 3 else None)
        return remote(ref, ref, self.sends, self.recvs, self.base + way * 4 + step, self.targets[way])

    def start(self, step):
        for way in (0, 1):
            copy = self.copy(way, step, 0)
            copy.start()
            self.started.append(copy)

    def wait(self, step):
        for way in (0, 1):
            self.copy(way, step, 1).wait_recv()

    def finish(self):
        for copy in self.started:
            copy.wait_send()


class Direct:
    def __init__(self, source, target, arrived, me, at, sends, recvs, base):
        self.source, self.target, self.arrived, self.me, self.at = source, target, arrived, me, at
        self.sends, self.recvs, self.base = sends, recvs, base
        self.started = []

    def start(self):
        for d in (4, 3, 5, 2, 6, 1, 7):
            index = lax.rem(self.me + d, 8)
            copy = remote(
                self.source(index), self.target(index, d), self.sends, self.recvs, self.base + d, self.at(d))
            copy.start()
            self.started.append(copy)

    def wait(self, d):
        ref = self.arrived(lax.rem(self.me + (8 - d), 8), d)
        remote(ref, ref, self.sends, self.recvs, self.base + d, self.at(d)).wait_recv()
        return ref

    def finish(self):
        for copy in self.started:
            copy.wait_send()


class ReduceRing:
    def __init__(self, own, inbox, me, right, left, sends, recvs, base):
        self.own, self.inbox, self.me, self.targets = own, inbox, me, (right, left)
        self.sends, self.recvs, self.base = sends, recvs, base
        self.started = []

    def index(self, way, step):
        offset = 4 - step if way == 0 else step + 4
        return lax.rem(self.me + offset, 8)

    def send(self, way, step, src):
        copy = remote(
            src, self.inbox(way, step), self.sends, self.recvs, self.base + way * 4 + step, self.targets[way]
        )
        copy.start()
        self.started.append(copy)

    def arrive(self, way, step):
        ref = self.inbox(way, step)
        remote(ref, ref, self.sends, self.recvs, self.base + way * 4 + step, self.targets[way]).wait_recv()

    def start(self):
        for way in (0, 1):
            self.send(way, 0, self.own(self.index(way, 0), way))

    def step(self, step):
        for way in (0, 1):
            self.arrive(way, step - 1)
            index = self.index(way, step)
            here = self.inbox(way, step - 1)
            if step == 1:
                part = self.own(index, way)
                part[...] = (part[...].astype(F32) + here[...].astype(F32)).astype(BF16)
                self.send(way, 1, self.own(index, None))
            else:
                here[...] = (here[...].astype(F32) + self.own(index, None)[...].astype(F32)).astype(BF16)
                self.send(way, step, here)

    def total(self):
        for way in (0, 1):
            self.arrive(way, 3)
        return (
            self.own(self.me, None)[...].astype(F32)
            + self.inbox(0, 3)[...].astype(F32)
            + self.inbox(1, 3)[...].astype(F32)
        )

    def finish(self):
        for copy in self.started:
            copy.wait_send()


def halves(ref, size, half):
    return ref if half is None else ref.at[pl.ds(half * size, size)]


def scratch(*shape, dtype=BF16):
    return pltpu.VMEM(shape, dtype)


PIECE = dict(
    keys=scratch(NY, NZ, LAT, HD),
    values=scratch(NZ, NY, LAT, HD),
    q_rows=scratch(2, TOK, HD),
    g_rows=scratch(2, TOK, HD),
    grad_q=scratch(2, TOK, HD),
    grad_keys=scratch(NY, NZ, LAT, HD),
    grad_values=scratch(NZ, NY, LAT, HD),
    key_in=scratch(2, 4, NZ, LAT, HD),
    value_in=scratch(2, 4, NY, LAT, HD),
    key_mid=scratch(NZ, LAT, HD),
    value_mid=scratch(NY, LAT, HD),
    key_low=scratch(NZ, LAT, HD),
    value_low=scratch(NY, LAT, HD),
    weights=scratch(2, NZ, NL, PAD, HD),
    weights_in=scratch(2, 2, 4, NL, PAD, HD),
    low_out=scratch(NL, PAD, 2 * HD),
    low_in=scratch(NL, PAD, 2 * HD),
    ring_send=pltpu.SemaphoreType.DMA((80,)),
    ring_recv=pltpu.SemaphoreType.DMA((80,)),
    swap_send=pltpu.SemaphoreType.DMA((28,)),
    swap_recv=pltpu.SemaphoreType.DMA((28,)),
    swap_own=pltpu.SemaphoreType.DMA((4,)),
    back_send=pltpu.SemaphoreType.DMA((14,)),
    back_recv=pltpu.SemaphoreType.DMA((14,)),
    back_own=pltpu.SemaphoreType.DMA((2,)),
    low_send=pltpu.SemaphoreType.DMA((4,)),
    low_recv=pltpu.SemaphoreType.DMA((4,)),
)
SHARED = dict(
    latents=scratch(LAT, VD),
    key_weight=scratch(VD, COLS),
    value_weight=scratch(VD, COLS),
    raw=scratch(LAT, COLS, dtype=F32),
    key_tile=scratch(LIST * LAT, HD),
    value_tile=scratch(LIST * LAT, HD),
    key_sums=scratch(2, 2, LIST + 1, LAT, HD, dtype=F32),
    value_sums=scratch(2, 2, LIST + 1, LAT, HD, dtype=F32),
    shares=scratch(2 * NX, PAD, HD),
    shares_in=scratch(2 * NX, PAD, HD),
    spread=scratch(2 * NX, PAD, HD, dtype=F32),
    wide=scratch(LAT, VD, dtype=F32),
    load_sem=pltpu.SemaphoreType.DMA((3,)),
    head_send=pltpu.SemaphoreType.DMA((16,)),
    head_recv=pltpu.SemaphoreType.DMA((16,)),
)


class Refs:
    def __init__(self, names, refs):
        self.__dict__.update(zip(names, refs))


def inbox(buffer, size):
    def place(way, step):
        ref = buffer.at[way, step]
        return ref.at[pl.ds(way * size, size)] if step == 0 else ref

    return place


def gather_rings(me, p):
    y, z = (me.at_y(1), me.at_y(-1)), (me.at_z(1), me.at_z(-1))
    sems = (p.ring_send, p.ring_recv)
    first = (
        Direct(
            lambda b: p.keys.at[me.y, me.z], lambda b, d: p.keys.at[me.y, me.z], lambda b, d: p.keys.at[me.y, b],
            me.z, me.at_z, *sems, 0),
        Direct(
            lambda b: p.values.at[me.z, me.y], lambda b, d: p.values.at[me.z, me.y],
            lambda b, d: p.values.at[me.z, b], me.y, me.at_y, *sems, 8),
    )
    second = (
        GatherRing(lambda b, half: halves(p.keys.at[b], NZ // 2, half), me.y, *y, *sems, 16),
        GatherRing(lambda b, half: halves(p.values.at[b], NY // 2, half), me.z, *z, *sems, 24),
    )
    return first, second


def reduce_rings(me, p):
    y, z = (me.at_y(1), me.at_y(-1)), (me.at_z(1), me.at_z(-1))
    sems = (p.ring_send, p.ring_recv)
    key_y = ReduceRing(
        lambda b, half: halves(p.grad_keys.at[b], NZ // 2, half), inbox(p.key_in, NZ // 2), me.y, *y, *sems, 32)
    value_z = ReduceRing(
        lambda b, half: halves(p.grad_values.at[b], NY // 2, half), inbox(p.value_in, NY // 2), me.z, *z, *sems, 40)
    key_z = Direct(
        lambda b: p.key_mid.at[b], lambda b, d: p.key_low.at[d], lambda b, d: p.key_low.at[d], me.z, me.at_z, *sems, 48)
    value_y = Direct(
        lambda b: p.value_mid.at[b], lambda b, d: p.value_low.at[d], lambda b, d: p.value_low.at[d],
        me.y, me.at_y, *sems, 56)
    weight_z = [
        ReduceRing(
            lambda b, half, k=k: halves(p.weights.at[k, b], NL // 2, half), inbox(p.weights_in.at[k], NL // 2),
            me.z, *z, *sems, 64 + 8 * k)
        for k in range(2)
    ]
    return [key_y, value_z, key_z, value_y] + weight_z


def columns(c, place, h):
    return pl.ds(pl.multiple_of((c * NX + place) * COLS + h * HD, HD), HD)


def rows_of(place):
    return pl.ds(pl.multiple_of(place * OWN, OWN), OWN)


class Swap:
    def __init__(self, me, p, h, queries, out_grad):
        self.me, self.p = me, p
        self.sent, self.own = [], []
        for d in range(NX):
            to = lax.rem(me.xc + d, NX)
            for n, (src, dst) in enumerate(((queries, p.q_rows), (out_grad, p.g_rows))):
                for c in range(2):
                    src_ref = src.at[:, columns(c, to, h)]
                    dst_ref = dst.at[c, rows_of(me.xc)]
                    if d == 0:
                        copy = pltpu.make_async_copy(src_ref, dst_ref, p.swap_own.at[n * 2 + c])
                        self.own.append(copy)
                    else:
                        sem = (d - 1) * 4 + n * 2 + c
                        copy = remote(src_ref, dst_ref, p.swap_send, p.swap_recv, sem, me.at_x(d))
                        self.sent.append(copy)
                    copy.start()

    def wait(self):
        me, p = self.me, self.p
        for d in range(1, NX):
            source = lax.rem(me.xc + (NX - d), NX)
            for n, dst in enumerate((p.q_rows, p.g_rows)):
                for c in range(2):
                    ref = dst.at[c, rows_of(source)]
                    sem = (d - 1) * 4 + n * 2 + c
                    remote(ref, ref, p.swap_send, p.swap_recv, sem, me.at_x(d)).wait_recv()
        for copy in self.own:
            copy.wait()

    def finish(self):
        for copy in self.sent:
            copy.wait_send()


class SwapBack:
    def __init__(self, me, p, h, out):
        self.me, self.p, self.h, self.out = me, p, h, out
        self.sent, self.own = [], []
        for d in range(NX):
            to = lax.rem(me.xc + d, NX)
            for c in range(2):
                src_ref = p.grad_q.at[c, rows_of(to)]
                dst_ref = out.at[:, columns(c, me.xc, h)]
                if d == 0:
                    copy = pltpu.make_async_copy(src_ref, dst_ref, p.back_own.at[c])
                    self.own.append(copy)
                else:
                    copy = remote(src_ref, dst_ref, p.back_send, p.back_recv, (d - 1) * 2 + c, me.at_x(d))
                    self.sent.append(copy)
                copy.start()

    def finish(self):
        me, p = self.me, self.p
        for d in range(1, NX):
            source = lax.rem(me.xc + (NX - d), NX)
            for c in range(2):
                ref = self.out.at[:, columns(c, source, self.h)]
                remote(ref, ref, p.back_send, p.back_recv, (d - 1) * 2 + c, me.at_x(d)).wait_recv()
        for copy in self.own:
            copy.wait()
        for copy in self.sent:
            copy.wait_send()


def attend(me, p, s, t, c, entries, gate, gain):
    for e in range(LIST):
        rows = slice(e * LAT, (e + 1) * LAT)
        slot = entries[t][e][0]
        s.key_tile[rows, :] = p.keys[c * NL + lax.div(slot, NZ), lax.rem(slot, NZ)]
        s.value_tile[rows, :] = p.values[lax.rem(slot, NZ), c * NL + lax.div(slot, NZ)]
    kt = s.key_tile[...]
    vt = s.value_tile[...]
    base = t * TILE
    q = p.q_rows[c, base:base + TILE, :].astype(F32)
    g = p.g_rows[c, base:base + TILE, :].astype(F32)
    inverse = lax.rsqrt(jnp.mean(q * q, axis=1, keepdims=True) + EPS)
    q_hat = (q * inverse * gain).astype(BF16)
    ctx = (gate * g).astype(BF16)
    scores = dot(kt, q_hat, 1, 1)
    grad_probs = dot(vt, ctx, 1, 1)
    token = me.seq * (2 * TOK) + me.yh * TOK + base + lax.broadcasted_iota(jnp.int32, (1, TILE), 1)
    total = jnp.zeros((1, TILE), F32)
    inner = jnp.zeros((1, TILE), F32)
    dead = jnp.ones((1, TILE), F32)
    exps = []
    for e in range(LIST):
        rows = slice(e * LAT, (e + 1) * LAT)
        live = entries[t][e][1] < token
        dead = jnp.where(live, 0.0, dead)
        x = jnp.where(live, jnp.exp2(scores[rows] * (SCALE * LOG2E)), 0.0)
        exps.append(x)
        total = total + jnp.sum(x, axis=0, keepdims=True)
        inner = inner + jnp.sum(x * grad_probs[rows], axis=0, keepdims=True)
    norm = 1.0 / (total + dead)
    inner = inner * norm
    probs = []
    grads = []
    for e in range(LIST):
        rows = slice(e * LAT, (e + 1) * LAT)
        prob = exps[e] * norm
        probs.append(prob.astype(BF16))
        grads.append((prob * (grad_probs[rows] - inner)).astype(BF16))
    probs = jnp.concatenate(probs, axis=0)
    grads = jnp.concatenate(grads, axis=0)
    s.key_sums[t, c, 0:LIST] = (dot(grads, q_hat, 1, 0) * SCALE).reshape(LIST, LAT, HD)
    s.value_sums[t, c, 0:LIST] = dot(probs, ctx, 1, 0).reshape(LIST, LAT, HD)
    up = dot(kt.T, grads, 1, 0).T * SCALE * gain
    row_inner = jnp.mean(up * q, axis=1, keepdims=True)
    p.grad_q[c, base:base + TILE, :] = (inverse * (up - q * (inverse * inverse * row_inner))).astype(BF16)


def to_slots(p, s, entries):
    def one_slot(slot, carry):
        z = lax.rem(slot, NZ)
        low = lax.div(slot, NZ)
        place = []
        for t in range(2):
            found = jnp.int32(LIST)
            for e in range(LIST):
                found = jnp.where(entries[t][e][2] == slot, e, found)
            place.append(found)
        for c in range(2):
            p.grad_keys[c * NL + low, z] = (
                s.key_sums[0, c, place[0]] + s.key_sums[1, c, place[1]]).astype(BF16)
            p.grad_values[z, c * NL + low] = (
                s.value_sums[0, c, place[0]] + s.value_sums[1, c, place[1]]).astype(BF16)
        return carry

    lax.fori_loop(0, SLOTS, one_slot, 0)


def kernel(
    tile_list, media_slot, media_position, gate_alpha,
    queries, out_grad, latents, key_weight, value_weight, query_gain, key_gain,
    out_queries, out_latents, out_key_weight, out_value_weight,
    *refs,
):
    count = len(PIECE)
    pieces = [Refs(PIECE, refs[h * count:(h + 1) * count]) for h in range(2)]
    s = Refs(SHARED, refs[2 * count:])
    me = Place()
    loads = [
        pltpu.make_async_copy(src, dst, s.load_sem.at[n])
        for n, (src, dst) in enumerate(
            ((latents, s.latents), (key_weight, s.key_weight), (value_weight, s.value_weight)))
    ]
    for load in loads:
        load.start()
    greet(
        [me.at_y(d) for d in range(1, NY)]
        + [me.at_z(d) for d in range(1, NZ)]
        + [me.at_head(d) for d in range(1, 2 * NX)]
    )
    for load in loads:
        load.wait()

    gain_k = key_gain[...]
    flat = s.latents[...]
    s.raw[...] = jnp.dot(flat, s.key_weight[...], preferred_element_type=F32)
    own_values = jnp.dot(flat, s.value_weight[...], preferred_element_type=F32).astype(BF16)
    for h, p in enumerate(pieces):
        cols = slice(h * HD, (h + 1) * HD)
        part = s.raw[:, cols]
        inverse = lax.rsqrt(jnp.mean(part * part, axis=1, keepdims=True) + EPS)
        p.keys[me.y, me.z] = (part * inverse * gain_k).astype(BF16)
        p.values[me.z, me.y] = own_values[:, cols]

    firsts, seconds = zip(*[gather_rings(me, p) for p in pieces])

    def start(rings, step):
        for ring in rings:
            ring.start(step)

    def follow(rings, step):
        for ring in rings:
            ring.wait(step)
            if step < 3:
                ring.start(step + 1)

    for rings in firsts:
        for ring in rings:
            ring.start()
    swaps = [Swap(me, pieces[0], 0, queries, out_grad)]

    entries = []
    for t in range(2):
        entries.append([])
        for e in range(LIST):
            image = tile_list[me.yh * 2 + t, e]
            held = jnp.maximum(image, 0)
            slot = media_slot[held]
            entries[t].append((
                slot,
                jnp.where(image >= 0, media_position[held], DEAD),
                jnp.where(image >= 0, slot, SLOTS),
            ))
    gate = jnp.tanh(jnp.full((1, HD), gate_alpha[0], F32))
    gain_q = query_gain[...]
    for t in range(2):
        for c in range(2):
            s.key_sums[t, c, LIST] = jnp.zeros((LAT, HD), F32)
            s.value_sums[t, c, LIST] = jnp.zeros((LAT, HD), F32)

    for rings, later in zip(firsts, seconds):
        for ring in rings:
            for d in range(1, 8):
                ring.wait(d)
        if rings is firsts[0]:
            start(later, 0)
    follow(seconds[0], 0)
    follow(seconds[0], 1)
    start(seconds[1], 0)
    swaps.append(Swap(me, pieces[1], 1, queries, out_grad))
    follow(seconds[0], 2)
    follow(seconds[1], 0)
    follow(seconds[0], 3)
    follow(seconds[1], 1)

    units = [(t, c) for t in range(2) for c in range(2)]

    def run(h, n):
        t, c = units[n]
        attend(me, pieces[h], s, t, c, entries, gate, gain_q)

    swaps[0].wait()
    run(0, 0)
    run(0, 1)
    follow(seconds[1], 2)
    run(0, 2)
    run(0, 3)
    to_slots(pieces[0], s, entries)
    sums = [reduce_rings(me, p) for p in pieces]
    raw_grads, value_grads, low_copies, head_copies = {}, {}, [], []

    def tasks(h):
        p = pieces[h]
        key_y, value_z, key_z, value_y, *weight_z = sums[h]

        def begin():
            key_y.start()
            value_z.start()

        def first(step):
            def act():
                key_y.step(step)
                value_z.step(step)
            return act

        def turn():
            p.key_mid[...] = key_y.total().astype(BF16)
            key_z.start()
            p.value_mid[...] = value_z.total().astype(BF16)
            value_y.start()

        def own_image():
            key_sum = p.key_mid[me.z].astype(F32)
            for d in (1, 7, 2, 6, 3, 5, 4):
                key_sum = key_sum + key_z.wait(d)[...].astype(F32)
            value_sum = p.value_mid[me.y].astype(F32)
            for d in (1, 7, 2, 6, 3, 5, 4):
                value_sum = value_sum + value_y.wait(d)[...].astype(F32)
            part = s.raw[:, h * HD:(h + 1) * HD]
            inverse = lax.rsqrt(jnp.mean(part * part, axis=1, keepdims=True) + EPS)
            up = key_sum * gain_k
            row_inner = jnp.mean(up * part, axis=1, keepdims=True)
            raw_grads[h] = (inverse * (up - part * (inverse * inverse * row_inner))).astype(BF16)
            value_grads[h] = value_sum.astype(BF16)
            for k, grad in enumerate((raw_grads[h], value_grads[h])):
                share = dot(s.latents[...], grad, 0, 0)
                for n in range(SLOTS):
                    block = share[n * 40:(n + 1) * 40]
                    block = jnp.concatenate([block, jnp.zeros((PAD - 40, HD), F32)], axis=0)
                    p.weights[k, n % NZ, n // NZ] = block.astype(BF16)
                weight_z[k].start()
            if h == 1:
                latent_share()

        def third(step):
            def act():
                for ring in weight_z:
                    ring.step(step)
            return act

        def low():
            for k, ring in enumerate(weight_z):
                p.low_out[:, :, k * HD:(k + 1) * HD] = ring.total().astype(BF16)
            for d in range(1, NL):
                copy = remote(
                    p.low_out.at[lax.rem(me.yl + d, NL)], p.low_in.at[d], p.low_send, p.low_recv, d, me.at_low(d))
                copy.start()
                low_copies.append(copy)

        def last():
            total = p.low_out[me.yl].astype(F32)
            for d in range(1, NL):
                ref = p.low_in.at[d]
                remote(ref, ref, p.low_send, p.low_recv, d, me.at_low(d)).wait_recv()
                total = total + ref[...].astype(F32)
            cols = slice(h * HD, (h + 1) * HD)
            out_key_weight[:, cols] = total[0:40, 0:HD]
            out_value_weight[:, cols] = total[0:40, HD:]

        return (
            [begin] + [first(step) for step in (1, 2, 3)] + [turn, own_image]
            + [third(step) for step in (1, 2, 3)] + [low, last]
        )

    def latent_share():
        raw_grad = jnp.concatenate([raw_grads[0], raw_grads[1]], axis=1)
        value_grad = jnp.concatenate([value_grads[0], value_grads[1]], axis=1)
        s.wide[...] = dot(raw_grad, s.key_weight[...], 1, 1) + dot(value_grad, s.value_weight[...], 1, 1)
        s.spread[...] = jnp.zeros_like(s.spread)
        for d in range(2 * NX):
            for n in range(VD // HD):
                s.spread[d, 4 * n:4 * n + 4, :] = s.wide[4 * d:4 * d + 4, n * HD:(n + 1) * HD]
        s.shares[...] = s.spread[...].astype(BF16)
        for d in range(1, 2 * NX):
            copy = remote(
                s.shares.at[lax.rem(me.head + d, 2 * NX)], s.shares_in.at[d], s.head_send, s.head_recv, d,
                me.at_head(d))
            copy.start()
            head_copies.append(copy)

    left = [tasks(0), tasks(1)]

    def go(h):
        left[h].pop(0)()

    go(0)
    backs = [SwapBack(me, pieces[0], 0, out_queries)]
    follow(seconds[1], 3)
    swaps[1].wait()
    run(1, 0)
    run(1, 1)
    go(0)
    run(1, 2)
    run(1, 3)
    to_slots(pieces[1], s, entries)
    go(1)
    go(0)
    backs.append(SwapBack(me, pieces[1], 1, out_queries))
    while left[1]:
        go(1)
        if left[0]:
            go(0)

    total = s.shares[me.head].astype(F32)
    for d in range(1, 2 * NX):
        ref = s.shares_in.at[d]
        remote(ref, ref, s.head_send, s.head_recv, d, me.at_head(d)).wait_recv()
        total = total + ref[...].astype(F32)
    s.spread[0] = total
    for n in range(VD // HD):
        s.wide[0:4, n * HD:(n + 1) * HD] = s.spread[0, 4 * n:4 * n + 4, :]
    out_latents[...] = s.wide[0:4, :].astype(BF16)

    for swap in swaps + backs:
        swap.finish()
    for copy in head_copies + low_copies:
        copy.wait_send()
    for rings in firsts + seconds + tuple(sums):
        for ring in rings:
            ring.finish()


VMEM = pl.BlockSpec(memory_space=pltpu.VMEM)
SMEM = pl.BlockSpec(memory_space=pltpu.SMEM)
HBM = pl.BlockSpec(memory_space=pl.ANY)
LIMIT = 60 * 1024 * 1024


def struct(shape, dtype):
    return jax.ShapeDtypeStruct(shape, dtype)


def body(
    queries,
    out_grad,
    latents,
    key_weight,
    value_weight,
    query_gain,
    key_gain,
    gate_alpha,
    media_slot,
    media_position,
    tile_list,
):
    query_grad, latent_grad, key_weight_grad, value_weight_grad = pl.pallas_call(
        kernel,
        out_shape=(
            struct((OWN, 2 * NX * COLS), BF16),
            struct((4, VD), BF16),
            struct((VD // SLOTS, COLS), F32),
            struct((VD // SLOTS, COLS), F32),
        ),
        in_specs=[SMEM] * 4 + [HBM] * 5 + [VMEM] * 2,
        out_specs=(HBM, VMEM, VMEM, VMEM),
        scratch_shapes=list(PIECE.values()) * 2 + list(SHARED.values()),
        compiler_params=pltpu.CompilerParams(collective_id=0, has_side_effects=True, vmem_limit_bytes=LIMIT),
        name="backward",
    )(
        tile_list, media_slot, media_position, gate_alpha,
        queries, out_grad, latents.reshape(LAT, VD), key_weight, value_weight,
        query_gain.reshape(1, HD), key_gain.reshape(1, HD),
    )
    return (query_grad, latent_grad.reshape(1, 4, VD), key_weight_grad, value_weight_grad)


def solution(mesh):
    in_specs = (
        P(("seq", "head"), None),
        P(("seq", "head"), None),
        P("seq", None, None),
        P(None, "head"),
        P(None, "head"),
        P(),
        P(),
        P(),
        P(),
        P(),
        P("seq", None),
    )
    out_specs = (
        P(("seq", "head"), None),
        P("seq", "head", None),
        P("seq", "head"),
        P("seq", "head"),
    )
    return jax.shard_map(body, mesh=mesh, in_specs=in_specs, out_specs=out_specs, check_vma=False)
```

```python
import jax
import jax.numpy as jnp
from jax import lax
from jax.experimental import pallas as pl
from jax.experimental.pallas import tpu as pltpu
from jax.sharding import PartitionSpec as P

HD = 128
EPS = 1e-06
SCALE = HD ** (-0.5)
LOG2E = 1.4426950408889634
MESH = pl.DeviceIdType.MESH

NZ = 8
NL = 4
NY = 8
NX = 8
LAT = 64
LIST = 8
TILE = 512
TOK = 1024
OWN = 128
COLS = 256
VD = 1280
PAD = 48
SLOTS = 32
DEAD = 1 << 30

F32 = jnp.float32
BF16 = jnp.bfloat16


def dot(a, b, ca, cb):
    return lax.dot_general(a, b, (((ca,), (cb,)), ((), ())), preferred_element_type=F32)


class Place:
    def __init__(self):
        self.seq = lax.axis_index("seq")
        self.head = lax.axis_index("head")
        self.z = lax.rem(self.seq, NZ)
        self.yl = lax.div(self.seq, NZ)
        self.yh = lax.div(self.head, NX)
        self.xc = lax.rem(self.head, NX)
        self.y = self.yh * NL + self.yl

    def at_y(self, step):
        y = lax.rem(self.y + (step + NY), NY)
        return (lax.rem(y, NL) * NZ + self.z, lax.div(y, NL) * NX + self.xc)

    def at_z(self, step):
        z = lax.rem(self.z + (step + NZ), NZ)
        return (self.yl * NZ + z, self.head)

    def at_x(self, step):
        return (self.seq, self.yh * NX + lax.rem(self.xc + step, NX))

    def at_head(self, step):
        return (self.seq, lax.rem(self.head + step, 2 * NX))

    def at_low(self, step):
        return (lax.rem(self.yl + step, NL) * NZ + self.z, self.head)


def greet(partners):
    for partner in partners:
        pl.semaphore_signal(pltpu.get_barrier_semaphore(), inc=1, device_id=partner, device_id_type=MESH)
    return lambda: pl.semaphore_wait(pltpu.get_barrier_semaphore(), len(partners))


def remote(src, dst, sends, recvs, sem, device):
    return pltpu.make_async_remote_copy(
        src_ref=src,
        dst_ref=dst,
        send_sem=sends.at[sem],
        recv_sem=recvs.at[sem],
        device_id=device,
        device_id_type=MESH,
    )


class GatherRing:
    def __init__(self, block, me, right, left, sends, recvs, base):
        self.block, self.me, self.targets = block, me, (right, left)
        self.sends, self.recvs, self.base = sends, recvs, base
        self.started = []

    def copy(self, way, step, shift):
        offset = (-step - shift) if way == 0 else (step + shift)
        ref = self.block(lax.rem(self.me + (offset + 8), 8), way if step == 3 else None)
        return remote(ref, ref, self.sends, self.recvs, self.base + way * 4 + step, self.targets[way])

    def start(self, step):
        for way in (0, 1):
            copy = self.copy(way, step, 0)
            copy.start()
            self.started.append(copy)

    def wait(self, step):
        for way in (0, 1):
            self.copy(way, step, 1).wait_recv()

    def finish(self):
        for copy in self.started:
            copy.wait_send()


class Direct:
    def __init__(self, source, target, arrived, me, at, sends, recvs, base):
        self.source, self.target, self.arrived, self.me, self.at = source, target, arrived, me, at
        self.sends, self.recvs, self.base = sends, recvs, base
        self.started = []

    def start(self):
        for d in (4, 3, 5, 2, 6, 1, 7):
            index = lax.rem(self.me + d, 8)
            copy = remote(
                self.source(index), self.target(index, d), self.sends, self.recvs, self.base + d, self.at(d))
            copy.start()
            self.started.append(copy)

    def wait(self, d):
        ref = self.arrived(lax.rem(self.me + (8 - d), 8), d)
        remote(ref, ref, self.sends, self.recvs, self.base + d, self.at(d)).wait_recv()
        return ref

    def finish(self):
        for copy in self.started:
            copy.wait_send()


class ReduceRing:
    def __init__(self, own, inbox, me, right, left, sends, recvs, base):
        self.own, self.inbox, self.me, self.targets = own, inbox, me, (right, left)
        self.sends, self.recvs, self.base = sends, recvs, base
        self.started = []

    def index(self, way, step):
        offset = 4 - step if way == 0 else step + 4
        return lax.rem(self.me + offset, 8)

    def send(self, way, step, src):
        copy = remote(
            src, self.inbox(way, step), self.sends, self.recvs, self.base + way * 4 + step, self.targets[way]
        )
        copy.start()
        self.started.append(copy)

    def arrive(self, way, step):
        ref = self.inbox(way, step)
        remote(ref, ref, self.sends, self.recvs, self.base + way * 4 + step, self.targets[way]).wait_recv()

    def start(self):
        for way in (0, 1):
            self.send(way, 0, self.own(self.index(way, 0), way))

    def step(self, step):
        for way in (0, 1):
            self.arrive(way, step - 1)
            index = self.index(way, step)
            here = self.inbox(way, step - 1)
            if step == 1:
                part = self.own(index, way)
                part[...] = (part[...].astype(F32) + here[...].astype(F32)).astype(BF16)
                self.send(way, 1, self.own(index, None))
            else:
                here[...] = (here[...].astype(F32) + self.own(index, None)[...].astype(F32)).astype(BF16)
                self.send(way, step, here)

    def total(self):
        for way in (0, 1):
            self.arrive(way, 3)
        return (
            self.own(self.me, None)[...].astype(F32)
            + self.inbox(0, 3)[...].astype(F32)
            + self.inbox(1, 3)[...].astype(F32)
        )

    def finish(self):
        for copy in self.started:
            copy.wait_send()


def halves(ref, size, half):
    return ref if half is None else ref.at[pl.ds(half * size, size)]


def quarters(ref, part, half):
    return ref.at[pl.ds(part * 4, 4)] if half is None else ref.at[pl.ds(part * 4 + half * 2, 2)]


def scratch(*shape, dtype=BF16):
    return pltpu.VMEM(shape, dtype)


PIECE = dict(
    keys=scratch(NY, NZ, LAT, HD),
    values=scratch(NZ, NY, LAT, HD),
    q_rows=scratch(2, TOK, HD),
    g_rows=scratch(2, TOK, HD),
    grad_q=scratch(2, TOK, HD),
    grad_keys=scratch(NY, NZ, LAT, HD),
    grad_values=scratch(NZ, NY, LAT, HD),
    key_in=scratch(2, 2, 4, 4, LAT, HD),
    value_in=scratch(2, 2, 4, 4, LAT, HD),
    key_mid=scratch(NZ, LAT, HD),
    value_mid=scratch(NY, LAT, HD),
    key_low=scratch(NZ, LAT, HD),
    value_low=scratch(NY, LAT, HD),
    weights=scratch(2, NZ, NL, PAD, HD),
    weights_in=scratch(2, 2, 4, NL, PAD, HD),
    low_out=scratch(NL, PAD, 2 * HD),
    low_in=scratch(NL, PAD, 2 * HD),
    ring_send=pltpu.SemaphoreType.DMA((112,)),
    ring_recv=pltpu.SemaphoreType.DMA((112,)),
    swap_send=pltpu.SemaphoreType.DMA((28,)),
    swap_recv=pltpu.SemaphoreType.DMA((28,)),
    swap_own=pltpu.SemaphoreType.DMA((4,)),
    back_send=pltpu.SemaphoreType.DMA((14,)),
    back_recv=pltpu.SemaphoreType.DMA((14,)),
    back_own=pltpu.SemaphoreType.DMA((2,)),
    low_send=pltpu.SemaphoreType.DMA((4,)),
    low_recv=pltpu.SemaphoreType.DMA((4,)),
)
SHARED = dict(
    latents=scratch(LAT, VD),
    key_weight=scratch(VD, COLS),
    value_weight=scratch(VD, COLS),
    raw=scratch(LAT, COLS, dtype=F32),
    key_tile=scratch(LIST * LAT, HD),
    value_tile=scratch(LIST * LAT, HD),
    key_sums=scratch(2, 2, LIST + 1, LAT, HD, dtype=F32),
    value_sums=scratch(2, 2, LIST + 1, LAT, HD, dtype=F32),
    shares=scratch(2 * NX, PAD, HD),
    shares_in=scratch(2 * NX, PAD, HD),
    spread=scratch(2 * NX, PAD, HD, dtype=F32),
    wide=scratch(LAT, VD, dtype=F32),
    latents_t=scratch(VD, LAT),
    places=pltpu.SMEM((2, SLOTS), jnp.int32),
    load_sem=pltpu.SemaphoreType.DMA((3,)),
    head_send=pltpu.SemaphoreType.DMA((16,)),
    head_recv=pltpu.SemaphoreType.DMA((16,)),
)


class Refs:
    def __init__(self, names, refs):
        self.__dict__.update(zip(names, refs))


def inbox(buffer, size):
    def place(way, step):
        ref = buffer.at[way, step]
        return ref.at[pl.ds(way * size, size)] if step == 0 else ref

    return place


def gather_rings(me, p):
    y, z = (me.at_y(1), me.at_y(-1)), (me.at_z(1), me.at_z(-1))
    sems = (p.ring_send, p.ring_recv)
    first = (
        Direct(
            lambda b: p.keys.at[me.y, me.z], lambda b, d: p.keys.at[me.y, me.z], lambda b, d: p.keys.at[me.y, b],
            me.z, me.at_z, *sems, 0),
        Direct(
            lambda b: p.values.at[me.z, me.y], lambda b, d: p.values.at[me.z, me.y],
            lambda b, d: p.values.at[me.z, b], me.y, me.at_y, *sems, 8),
    )
    second = []
    for n in range(2):
        second += [
            GatherRing(lambda b, half, n=n: quarters(p.keys.at[b], n, half), me.y, *y, *sems, 16 + 8 * n),
            GatherRing(lambda b, half, n=n: quarters(p.values.at[b], n, half), me.z, *z, *sems, 32 + 8 * n),
        ]
    return first, second


def reduce_rings(me, p):
    y, z = (me.at_y(1), me.at_y(-1)), (me.at_z(1), me.at_z(-1))
    sems = (p.ring_send, p.ring_recv)
    key_y = [
        ReduceRing(
            lambda b, half, n=n: quarters(p.grad_keys.at[b], n, half), inbox(p.key_in.at[n], 2),
            me.y, *y, *sems, 48 + 8 * n)
        for n in range(2)
    ]
    value_z = [
        ReduceRing(
            lambda b, half, n=n: quarters(p.grad_values.at[b], n, half), inbox(p.value_in.at[n], 2),
            me.z, *z, *sems, 64 + 8 * n)
        for n in range(2)
    ]
    key_z = Direct(
        lambda b: p.key_mid.at[b], lambda b, d: p.key_low.at[d], lambda b, d: p.key_low.at[d], me.z, me.at_z, *sems, 80)
    value_y = Direct(
        lambda b: p.value_mid.at[b], lambda b, d: p.value_low.at[d], lambda b, d: p.value_low.at[d],
        me.y, me.at_y, *sems, 88)
    weight_z = [
        ReduceRing(
            lambda b, half, k=k: halves(p.weights.at[k, b], NL // 2, half), inbox(p.weights_in.at[k], NL // 2),
            me.z, *z, *sems, 96 + 8 * k)
        for k in range(2)
    ]
    return key_y, value_z, key_z, value_y, weight_z


def columns(c, place, h):
    return pl.ds(pl.multiple_of((c * NX + place) * COLS + h * HD, HD), HD)


def rows_of(place):
    return pl.ds(pl.multiple_of(place * OWN, OWN), OWN)


class Swap:
    def __init__(self, me, p, h, queries, out_grad):
        self.me, self.p = me, p
        self.sent, self.own = [], []
        for d in range(NX):
            to = lax.rem(me.xc + d, NX)
            for n, (src, dst) in enumerate(((queries, p.q_rows), (out_grad, p.g_rows))):
                for c in range(2):
                    src_ref = src.at[:, columns(c, to, h)]
                    dst_ref = dst.at[c, rows_of(me.xc)]
                    if d == 0:
                        copy = pltpu.make_async_copy(src_ref, dst_ref, p.swap_own.at[n * 2 + c])
                        self.own.append(copy)
                    else:
                        sem = (d - 1) * 4 + n * 2 + c
                        copy = remote(src_ref, dst_ref, p.swap_send, p.swap_recv, sem, me.at_x(d))
                        self.sent.append(copy)
                    copy.start()

    def wait(self):
        me, p = self.me, self.p
        for d in range(1, NX):
            source = lax.rem(me.xc + (NX - d), NX)
            for n, dst in enumerate((p.q_rows, p.g_rows)):
                for c in range(2):
                    ref = dst.at[c, rows_of(source)]
                    sem = (d - 1) * 4 + n * 2 + c
                    remote(ref, ref, p.swap_send, p.swap_recv, sem, me.at_x(d)).wait_recv()
        for copy in self.own:
            copy.wait()

    def finish(self):
        for copy in self.sent:
            copy.wait_send()


class SwapBack:
    def __init__(self, me, p, h, out):
        self.me, self.p, self.h, self.out = me, p, h, out
        self.sent, self.own = [], []
        for d in range(NX):
            to = lax.rem(me.xc + d, NX)
            for c in range(2):
                src_ref = p.grad_q.at[c, rows_of(to)]
                dst_ref = out.at[:, columns(c, me.xc, h)]
                if d == 0:
                    copy = pltpu.make_async_copy(src_ref, dst_ref, p.back_own.at[c])
                    self.own.append(copy)
                else:
                    copy = remote(src_ref, dst_ref, p.back_send, p.back_recv, (d - 1) * 2 + c, me.at_x(d))
                    self.sent.append(copy)
                copy.start()

    def finish(self):
        me, p = self.me, self.p
        for d in range(1, NX):
            source = lax.rem(me.xc + (NX - d), NX)
            for c in range(2):
                ref = self.out.at[:, columns(c, source, self.h)]
                remote(ref, ref, p.back_send, p.back_recv, (d - 1) * 2 + c, me.at_x(d)).wait_recv()
        for copy in self.own:
            copy.wait()
        for copy in self.sent:
            copy.wait_send()


def attend(me, p, s, t, c, entries, gate, gain):
    for e in range(LIST):
        rows = slice(e * LAT, (e + 1) * LAT)
        slot = entries[t][e][0]
        s.key_tile[rows, :] = p.keys[c * NL + lax.div(slot, NZ), lax.rem(slot, NZ)]
        s.value_tile[rows, :] = p.values[lax.rem(slot, NZ), c * NL + lax.div(slot, NZ)]
    kt = s.key_tile[...]
    vt = s.value_tile[...]
    base = t * TILE
    q = p.q_rows[c, base:base + TILE, :].astype(F32)
    g = p.g_rows[c, base:base + TILE, :].astype(F32)
    inverse = lax.rsqrt(jnp.mean(q * q, axis=1, keepdims=True) + EPS)
    q_hat = (q * inverse * gain).astype(BF16)
    ctx = (gate * g).astype(BF16)
    scores = dot(kt, q_hat, 1, 1)
    grad_probs = dot(vt, ctx, 1, 1)
    token = me.seq * (2 * TOK) + me.yh * TOK + base + lax.broadcasted_iota(jnp.int32, (1, TILE), 1)
    total = jnp.zeros((1, TILE), F32)
    inner = jnp.zeros((1, TILE), F32)
    dead = jnp.ones((1, TILE), F32)
    exps = []
    for e in range(LIST):
        rows = slice(e * LAT, (e + 1) * LAT)
        live = entries[t][e][1] < token
        dead = jnp.where(live, 0.0, dead)
        x = jnp.where(live, jnp.exp2(scores[rows] * (SCALE * LOG2E)), 0.0)
        exps.append(x)
        total = total + jnp.sum(x, axis=0, keepdims=True)
        inner = inner + jnp.sum(x * grad_probs[rows], axis=0, keepdims=True)
    norm = 1.0 / (total + dead)
    inner = inner * norm
    probs = []
    grads = []
    for e in range(LIST):
        rows = slice(e * LAT, (e + 1) * LAT)
        prob = exps[e] * norm
        probs.append(prob.astype(BF16))
        grads.append((prob * (grad_probs[rows] - inner)).astype(BF16))
    probs = jnp.concatenate(probs, axis=0)
    grads = jnp.concatenate(grads, axis=0)
    s.key_sums[t, c, 0:LIST] = (dot(grads, q_hat, 1, 0) * SCALE).reshape(LIST, LAT, HD)
    s.value_sums[t, c, 0:LIST] = dot(probs, ctx, 1, 0).reshape(LIST, LAT, HD)
    up = dot(kt.T, grads, 1, 0).T * SCALE * gain
    row_inner = jnp.mean(up * q, axis=1, keepdims=True)
    p.grad_q[c, base:base + TILE, :] = (inverse * (up - q * (inverse * inverse * row_inner))).astype(BF16)


def find_places(places, entries):
    def one_slot(slot, carry):
        for t in range(2):
            found = jnp.int32(LIST)
            for e in range(LIST):
                found = jnp.where(entries[t][e][2] == slot, e, found)
            places[t, slot] = found
        return carry

    lax.fori_loop(0, SLOTS, one_slot, 0)


def to_slots(tile_sums, places, target):
    def one_slot(slot, carry):
        for c in range(2):
            target(c, lax.div(slot, NZ), lax.rem(slot, NZ))[...] = (
                tile_sums[0, c, places[0, slot]] + tile_sums[1, c, places[1, slot]]).astype(BF16)
        return carry

    lax.fori_loop(0, SLOTS, one_slot, 0)


def kernel(
    tile_list, media_slot, media_position, gate_alpha,
    queries, out_grad, latents, key_weight, value_weight, query_gain, key_gain,
    out_queries, out_latents, out_key_weight, out_value_weight,
    *refs,
):
    count = len(PIECE)
    pieces = [Refs(PIECE, refs[h * count:(h + 1) * count]) for h in range(2)]
    s = Refs(SHARED, refs[2 * count:])
    me = Place()
    loads = [
        pltpu.make_async_copy(src, dst, s.load_sem.at[n])
        for n, (src, dst) in enumerate(
            ((latents, s.latents), (key_weight, s.key_weight), (value_weight, s.value_weight)))
    ]
    for load in loads:
        load.start()
    wait_for_all = greet(
        [me.at_y(d) for d in range(1, NY)]
        + [me.at_z(d) for d in range(1, NZ)]
        + [me.at_head(d) for d in range(1, 2 * NX)]
    )
    for load in loads:
        load.wait()

    gain_k = key_gain[...]
    flat = s.latents[...]
    s.raw[...] = jnp.dot(flat, s.key_weight[...], preferred_element_type=F32)
    own_values = jnp.dot(flat, s.value_weight[...], preferred_element_type=F32).astype(BF16)
    for h, p in enumerate(pieces):
        cols = slice(h * HD, (h + 1) * HD)
        part = s.raw[:, cols]
        inverse = lax.rsqrt(jnp.mean(part * part, axis=1, keepdims=True) + EPS)
        p.keys[me.y, me.z] = (part * inverse * gain_k).astype(BF16)
        p.values[me.z, me.y] = own_values[:, cols]

    wait_for_all()

    firsts, seconds = zip(*[gather_rings(me, p) for p in pieces])

    def start(rings, step):
        for ring in rings:
            ring.start(step)

    def follow(rings, step):
        for ring in rings:
            ring.wait(step)
            if step < 3:
                ring.start(step + 1)

    for rings in firsts:
        for ring in rings:
            ring.start()
    swaps = [Swap(me, pieces[0], 0, queries, out_grad)]

    entries = []
    for t in range(2):
        entries.append([])
        for e in range(LIST):
            image = tile_list[me.yh * 2 + t, e]
            held = jnp.maximum(image, 0)
            slot = media_slot[held]
            entries[t].append((
                slot,
                jnp.where(image >= 0, media_position[held], DEAD),
                jnp.where(image >= 0, slot, SLOTS),
            ))
    gate = jnp.tanh(jnp.full((1, HD), gate_alpha[0], F32))
    gain_q = query_gain[...]
    for t in range(2):
        for c in range(2):
            s.key_sums[t, c, LIST] = jnp.zeros((LAT, HD), F32)
            s.value_sums[t, c, LIST] = jnp.zeros((LAT, HD), F32)

    find_places(s.places, entries)
    s.latents_t[...] = flat.astype(F32).T.astype(BF16)

    for rings, later in zip(firsts, seconds):
        for ring in rings:
            for d in range(1, 8):
                ring.wait(d)
        if rings is firsts[0]:
            start(later, 0)
    follow(seconds[0], 0)
    swaps.append(Swap(me, pieces[1], 1, queries, out_grad))
    follow(seconds[0], 1)
    follow(seconds[0], 2)
    start(seconds[1], 0)
    follow(seconds[0], 3)

    units = [(t, c) for t in range(2) for c in range(2)]

    def run(h, n):
        t, c = units[n]
        attend(me, pieces[h], s, t, c, entries, gate, gain_q)

    swaps[0].wait()
    for n in range(4):
        run(0, n)
        if n < 3:
            follow(seconds[1], n)
    sums = [reduce_rings(me, p) for p in pieces]
    raw_grads, value_grads, low_copies, head_copies = {}, {}, [], []

    def tasks(h):
        p = pieces[h]
        key_y, value_z, key_z, value_y, weight_z = sums[h]

        def begin():
            to_slots(s.key_sums, s.places, lambda c, low, z: p.grad_keys.at[c * NL + low, z])
            for ring in key_y:
                ring.start()
            to_slots(s.value_sums, s.places, lambda c, low, z: p.grad_values.at[z, c * NL + low])
            for ring in value_z:
                ring.start()

        def first(step):
            def act():
                for pair in zip(key_y, value_z):
                    for ring in pair:
                        ring.step(step)
            return act

        def turn():
            for n, ring in enumerate(key_y):
                p.key_mid[n * 4:n * 4 + 4] = ring.total().astype(BF16)
            key_z.start()
            for n, ring in enumerate(value_z):
                p.value_mid[n * 4:n * 4 + 4] = ring.total().astype(BF16)
            value_y.start()

        def own_image():
            key_sum = p.key_mid[me.z].astype(F32)
            for d in (1, 7, 2, 6, 3, 5, 4):
                key_sum = key_sum + key_z.wait(d)[...].astype(F32)
            value_sum = p.value_mid[me.y].astype(F32)
            for d in (1, 7, 2, 6, 3, 5, 4):
                value_sum = value_sum + value_y.wait(d)[...].astype(F32)
            part = s.raw[:, h * HD:(h + 1) * HD]
            inverse = lax.rsqrt(jnp.mean(part * part, axis=1, keepdims=True) + EPS)
            up = key_sum * gain_k
            row_inner = jnp.mean(up * part, axis=1, keepdims=True)
            raw_grads[h] = (inverse * (up - part * (inverse * inverse * row_inner))).astype(BF16)
            value_grads[h] = value_sum.astype(BF16)
            both = jnp.concatenate([raw_grads[h], value_grads[h]], axis=1)
            share = jnp.dot(s.latents_t[...], both, preferred_element_type=F32)
            for k in range(2):
                for n in range(SLOTS):
                    block = share[n * 40:(n + 1) * 40, k * HD:(k + 1) * HD]
                    block = jnp.concatenate([block, jnp.zeros((PAD - 40, HD), F32)], axis=0)
                    p.weights[k, n % NZ, n // NZ] = block.astype(BF16)
                weight_z[k].start()

        def third(step):
            def act():
                for ring in weight_z:
                    ring.step(step)
                if h == 1 and step == 1:
                    latent_share()
            return act

        def low():
            for k, ring in enumerate(weight_z):
                p.low_out[:, :, k * HD:(k + 1) * HD] = ring.total().astype(BF16)
            for d in range(1, NL):
                copy = remote(
                    p.low_out.at[lax.rem(me.yl + d, NL)], p.low_in.at[d], p.low_send, p.low_recv, d, me.at_low(d))
                copy.start()
                low_copies.append(copy)

        def last():
            total = p.low_out[me.yl].astype(F32)
            for d in range(1, NL):
                ref = p.low_in.at[d]
                remote(ref, ref, p.low_send, p.low_recv, d, me.at_low(d)).wait_recv()
                total = total + ref[...].astype(F32)
            cols = slice(h * HD, (h + 1) * HD)
            out_key_weight[:, cols] = total[0:40, 0:HD]
            out_value_weight[:, cols] = total[0:40, HD:]

        return (
            [begin] + [first(step) for step in (1, 2, 3)] + [turn, own_image]
            + [third(step) for step in (1, 2, 3)] + [low, last]
        )

    def latent_share():
        raw_grad = jnp.concatenate([raw_grads[0], raw_grads[1]], axis=1)
        value_grad = jnp.concatenate([value_grads[0], value_grads[1]], axis=1)
        s.wide[...] = dot(raw_grad, s.key_weight[...], 1, 1) + dot(value_grad, s.value_weight[...], 1, 1)
        s.spread[...] = jnp.zeros_like(s.spread)
        for d in range(2 * NX):
            for n in range(VD // HD):
                s.spread[d, 4 * n:4 * n + 4, :] = s.wide[4 * d:4 * d + 4, n * HD:(n + 1) * HD]
        s.shares[...] = s.spread[...].astype(BF16)
        for d in range(1, 2 * NX):
            copy = remote(
                s.shares.at[lax.rem(me.head + d, 2 * NX)], s.shares_in.at[d], s.head_send, s.head_recv, d,
                me.at_head(d))
            copy.start()
            head_copies.append(copy)

    left = [tasks(0), tasks(1)]

    def go(h):
        left[h].pop(0)()

    go(0)
    backs = [SwapBack(me, pieces[0], 0, out_queries)]
    follow(seconds[1], 3)
    swaps[1].wait()
    run(1, 0)
    run(1, 1)
    go(0)
    run(1, 2)
    run(1, 3)
    go(1)
    go(0)
    backs.append(SwapBack(me, pieces[1], 1, out_queries))
    while left[1]:
        go(1)
        if left[0]:
            go(0)

    total = s.shares[me.head].astype(F32)
    for d in range(1, 2 * NX):
        ref = s.shares_in.at[d]
        remote(ref, ref, s.head_send, s.head_recv, d, me.at_head(d)).wait_recv()
        total = total + ref[...].astype(F32)
    s.spread[0] = total
    for n in range(VD // HD):
        s.wide[0:4, n * HD:(n + 1) * HD] = s.spread[0, 4 * n:4 * n + 4, :]
    out_latents[...] = s.wide[0:4, :].astype(BF16)

    for swap in swaps + backs:
        swap.finish()
    for copy in head_copies + low_copies:
        copy.wait_send()
    for rings in firsts + seconds:
        for ring in rings:
            ring.finish()
    for key_y, value_z, key_z, value_y, weight_z in sums:
        for ring in key_y + value_z + [key_z, value_y] + weight_z:
            ring.finish()


def hand_on(*refs):
    sources, results, sems = refs[:4], refs[4:8], refs[8]
    copies = [
        pltpu.make_async_copy(src, dst, sems.at[n]) for n, (src, dst) in enumerate(zip(sources, results))
    ]
    for copy in copies:
        copy.start()
    for copy in copies:
        copy.wait()


VMEM = pl.BlockSpec(memory_space=pltpu.VMEM)
SMEM = pl.BlockSpec(memory_space=pltpu.SMEM)
HBM = pl.BlockSpec(memory_space=pl.ANY)
LIMIT = 60 * 1024 * 1024


def struct(shape, dtype):
    return jax.ShapeDtypeStruct(shape, dtype)


def body(
    queries,
    out_grad,
    latents,
    key_weight,
    value_weight,
    query_gain,
    key_gain,
    gate_alpha,
    media_slot,
    media_position,
    tile_list,
):
    shapes = (
        struct((OWN, 2 * NX * COLS), BF16),
        struct((4, VD), BF16),
        struct((VD // SLOTS, COLS), F32),
        struct((VD // SLOTS, COLS), F32),
    )
    grads = pl.pallas_call(
        kernel,
        out_shape=shapes,
        in_specs=[SMEM] * 4 + [HBM] * 5 + [VMEM] * 2,
        out_specs=(HBM, VMEM, VMEM, VMEM),
        scratch_shapes=list(PIECE.values()) * 2 + list(SHARED.values()),
        compiler_params=pltpu.CompilerParams(collective_id=0, has_side_effects=True, vmem_limit_bytes=LIMIT),
        name="backward",
    )(
        tile_list, media_slot, media_position, gate_alpha,
        queries, out_grad, latents.reshape(LAT, VD), key_weight, value_weight,
        query_gain.reshape(1, HD), key_gain.reshape(1, HD),
    )
    query_grad, latent_grad, key_weight_grad, value_weight_grad = pl.pallas_call(
        hand_on,
        out_shape=shapes,
        in_specs=[HBM] * 4,
        out_specs=(HBM,) * 4,
        scratch_shapes=[pltpu.SemaphoreType.DMA((4,))],
        compiler_params=pltpu.CompilerParams(vmem_limit_bytes=LIMIT),
        name="hand_on",
    )(*grads)
    return (query_grad, latent_grad.reshape(1, 4, VD), key_weight_grad, value_weight_grad)


def solution(mesh):
    in_specs = (
        P(("seq", "head"), None),
        P(("seq", "head"), None),
        P("seq", None, None),
        P(None, "head"),
        P(None, "head"),
        P(),
        P(),
        P(),
        P(),
        P(),
        P("seq", None),
    )
    out_specs = (
        P(("seq", "head"), None),
        P("seq", "head", None),
        P("seq", "head"),
        P("seq", "head"),
    )
    return jax.shard_map(body, mesh=mesh, in_specs=in_specs, out_specs=out_specs, check_vma=False)
```

```python
import jax
import jax.numpy as jnp
from jax import lax
from jax.experimental import pallas as pl
from jax.experimental.pallas import tpu as pltpu
from jax.sharding import PartitionSpec as P

HD = 128
EPS = 1e-06
SCALE = HD ** (-0.5)
LOG2E = 1.4426950408889634
MESH = pl.DeviceIdType.MESH

NZ = 8
NL = 4
NY = 8
NX = 8
LAT = 64
LIST = 8
TILE = 512
TOK = 1024
OWN = 128
COLS = 256
VD = 1280
PAD = 48
SLOTS = 32
DEAD = 1 << 30

F32 = jnp.float32
BF16 = jnp.bfloat16


def dot(a, b, ca, cb):
    return lax.dot_general(a, b, (((ca,), (cb,)), ((), ())), preferred_element_type=F32)


class Place:
    def __init__(self):
        self.seq = lax.axis_index("seq")
        self.head = lax.axis_index("head")
        self.z = lax.rem(self.seq, NZ)
        self.yl = lax.div(self.seq, NZ)
        self.yh = lax.div(self.head, NX)
        self.xc = lax.rem(self.head, NX)
        self.y = self.yh * NL + self.yl

    def at_y(self, step):
        y = lax.rem(self.y + (step + NY), NY)
        return (lax.rem(y, NL) * NZ + self.z, lax.div(y, NL) * NX + self.xc)

    def at_z(self, step):
        z = lax.rem(self.z + (step + NZ), NZ)
        return (self.yl * NZ + z, self.head)

    def at_x(self, step):
        return (self.seq, self.yh * NX + lax.rem(self.xc + step, NX))

    def at_head(self, step):
        return (self.seq, lax.rem(self.head + step, 2 * NX))

    def at_low(self, step):
        return (lax.rem(self.yl + step, NL) * NZ + self.z, self.head)


def greet(partners):
    for partner in partners:
        pl.semaphore_signal(pltpu.get_barrier_semaphore(), inc=1, device_id=partner, device_id_type=MESH)
    return lambda: pl.semaphore_wait(pltpu.get_barrier_semaphore(), len(partners))


def remote(src, dst, sends, recvs, sem, device):
    return pltpu.make_async_remote_copy(
        src_ref=src,
        dst_ref=dst,
        send_sem=sends.at[sem],
        recv_sem=recvs.at[sem],
        device_id=device,
        device_id_type=MESH,
    )


class GatherRing:
    def __init__(self, block, me, right, left, sends, recvs, base):
        self.block, self.me, self.targets = block, me, (right, left)
        self.sends, self.recvs, self.base = sends, recvs, base
        self.started = []

    def copy(self, way, step, shift):
        offset = (-step - shift) if way == 0 else (step + shift)
        ref = self.block(lax.rem(self.me + (offset + 8), 8), way if step == 3 else None)
        return remote(ref, ref, self.sends, self.recvs, self.base + way * 4 + step, self.targets[way])

    def start(self, step):
        for way in (0, 1):
            copy = self.copy(way, step, 0)
            copy.start()
            self.started.append(copy)

    def wait(self, step):
        for way in (0, 1):
            self.copy(way, step, 1).wait_recv()

    def finish(self):
        for copy in self.started:
            copy.wait_send()


class Direct:
    def __init__(self, source, target, arrived, me, at, sends, recvs, base):
        self.source, self.target, self.arrived, self.me, self.at = source, target, arrived, me, at
        self.sends, self.recvs, self.base = sends, recvs, base
        self.started = []

    def start(self):
        for d in (4, 3, 5, 2, 6, 1, 7):
            index = lax.rem(self.me + d, 8)
            copy = remote(
                self.source(index), self.target(index, d), self.sends, self.recvs, self.base + d, self.at(d))
            copy.start()
            self.started.append(copy)

    def wait(self, d):
        ref = self.arrived(lax.rem(self.me + (8 - d), 8), d)
        remote(ref, ref, self.sends, self.recvs, self.base + d, self.at(d)).wait_recv()
        return ref

    def finish(self):
        for copy in self.started:
            copy.wait_send()


class ReduceRing:
    def __init__(self, own, inbox, me, right, left, sends, recvs, base):
        self.own, self.inbox, self.me, self.targets = own, inbox, me, (right, left)
        self.sends, self.recvs, self.base = sends, recvs, base
        self.started = []

    def index(self, way, step):
        offset = 4 - step if way == 0 else step + 4
        return lax.rem(self.me + offset, 8)

    def send(self, way, step, src):
        copy = remote(
            src, self.inbox(way, step), self.sends, self.recvs, self.base + way * 4 + step, self.targets[way]
        )
        copy.start()
        self.started.append(copy)

    def arrive(self, way, step):
        ref = self.inbox(way, step)
        remote(ref, ref, self.sends, self.recvs, self.base + way * 4 + step, self.targets[way]).wait_recv()

    def start(self):
        for way in (0, 1):
            self.send(way, 0, self.own(self.index(way, 0), way))

    def step(self, step):
        for way in (0, 1):
            self.arrive(way, step - 1)
            index = self.index(way, step)
            here = self.inbox(way, step - 1)
            if step == 1:
                part = self.own(index, way)
                part[...] = (part[...].astype(F32) + here[...].astype(F32)).astype(BF16)
                self.send(way, 1, self.own(index, None))
            else:
                here[...] = (here[...].astype(F32) + self.own(index, None)[...].astype(F32)).astype(BF16)
                self.send(way, step, here)

    def total(self):
        for way in (0, 1):
            self.arrive(way, 3)
        return (
            self.own(self.me, None)[...].astype(F32)
            + self.inbox(0, 3)[...].astype(F32)
            + self.inbox(1, 3)[...].astype(F32)
        )

    def finish(self):
        for copy in self.started:
            copy.wait_send()


def halves(ref, size, half):
    return ref if half is None else ref.at[pl.ds(half * size, size)]


def quarters(ref, part, half):
    return ref.at[pl.ds(part * 4, 4)] if half is None else ref.at[pl.ds(part * 4 + half * 2, 2)]


def scratch(*shape, dtype=BF16):
    return pltpu.VMEM(shape, dtype)


PIECE = dict(
    keys=scratch(NY, NZ, LAT, HD),
    values=scratch(NZ, NY, LAT, HD),
    grad_keys=scratch(NY, NZ, LAT, HD),
    grad_values=scratch(NZ, NY, LAT, HD),
    key_in=scratch(2, 2, 4, 4, LAT, HD),
    value_in=scratch(2, 2, 4, 4, LAT, HD),
    key_mid=scratch(NZ, LAT, HD),
    value_mid=scratch(NY, LAT, HD),
    key_low=scratch(NZ, LAT, HD),
    value_low=scratch(NY, LAT, HD),
    weights=scratch(2, NZ, NL, PAD, HD),
    weights_in=scratch(2, 2, 4, NL, PAD, HD),
    low_out=scratch(NL, PAD, 2 * HD),
    low_in=scratch(NL, PAD, 2 * HD),
    ring_send=pltpu.SemaphoreType.DMA((112,)),
    ring_recv=pltpu.SemaphoreType.DMA((112,)),
    low_send=pltpu.SemaphoreType.DMA((4,)),
    low_recv=pltpu.SemaphoreType.DMA((4,)),
)
SHARED = dict(
    q_rows=scratch(2, TOK, COLS),
    g_rows=scratch(2, TOK, COLS),
    grad_q=scratch(2, TOK, COLS),
    swap_send=pltpu.SemaphoreType.DMA((28,)),
    swap_recv=pltpu.SemaphoreType.DMA((28,)),
    swap_own=pltpu.SemaphoreType.DMA((4,)),
    back_send=pltpu.SemaphoreType.DMA((14,)),
    back_recv=pltpu.SemaphoreType.DMA((14,)),
    back_own=pltpu.SemaphoreType.DMA((2,)),
    latents=scratch(LAT, VD),
    key_weight=scratch(VD, COLS),
    value_weight=scratch(VD, COLS),
    raw=scratch(LAT, COLS, dtype=F32),
    key_tile=scratch(LIST * LAT, HD),
    value_tile=scratch(LIST * LAT, HD),
    key_sums=scratch(2, 2, LIST + 1, LAT, HD, dtype=F32),
    value_sums=scratch(2, 2, LIST + 1, LAT, HD, dtype=F32),
    shares=scratch(2 * NX, PAD, HD),
    shares_in=scratch(2 * NX, PAD, HD),
    spread=scratch(2 * NX, PAD, HD, dtype=F32),
    wide=scratch(LAT, VD, dtype=F32),
    latents_t=scratch(VD, LAT),
    places=pltpu.SMEM((2, SLOTS), jnp.int32),
    load_sem=pltpu.SemaphoreType.DMA((3,)),
    head_send=pltpu.SemaphoreType.DMA((16,)),
    head_recv=pltpu.SemaphoreType.DMA((16,)),
)


class Refs:
    def __init__(self, names, refs):
        self.__dict__.update(zip(names, refs))


def inbox(buffer, size):
    def place(way, step):
        ref = buffer.at[way, step]
        return ref.at[pl.ds(way * size, size)] if step == 0 else ref

    return place


def gather_rings(me, p):
    y, z = (me.at_y(1), me.at_y(-1)), (me.at_z(1), me.at_z(-1))
    sems = (p.ring_send, p.ring_recv)
    first = (
        Direct(
            lambda b: p.keys.at[me.y, me.z], lambda b, d: p.keys.at[me.y, me.z], lambda b, d: p.keys.at[me.y, b],
            me.z, me.at_z, *sems, 0),
        Direct(
            lambda b: p.values.at[me.z, me.y], lambda b, d: p.values.at[me.z, me.y],
            lambda b, d: p.values.at[me.z, b], me.y, me.at_y, *sems, 8),
    )
    second = []
    for n in range(2):
        second += [
            GatherRing(lambda b, half, n=n: quarters(p.keys.at[b], n, half), me.y, *y, *sems, 16 + 8 * n),
            GatherRing(lambda b, half, n=n: quarters(p.values.at[b], n, half), me.z, *z, *sems, 32 + 8 * n),
        ]
    return first, second


def reduce_rings(me, p):
    y, z = (me.at_y(1), me.at_y(-1)), (me.at_z(1), me.at_z(-1))
    sems = (p.ring_send, p.ring_recv)
    key_y = [
        ReduceRing(
            lambda b, half, n=n: quarters(p.grad_keys.at[b], n, half), inbox(p.key_in.at[n], 2),
            me.y, *y, *sems, 48 + 8 * n)
        for n in range(2)
    ]
    value_z = [
        ReduceRing(
            lambda b, half, n=n: quarters(p.grad_values.at[b], n, half), inbox(p.value_in.at[n], 2),
            me.z, *z, *sems, 64 + 8 * n)
        for n in range(2)
    ]
    key_z = Direct(
        lambda b: p.key_mid.at[b], lambda b, d: p.key_low.at[d], lambda b, d: p.key_low.at[d], me.z, me.at_z, *sems, 80)
    value_y = Direct(
        lambda b: p.value_mid.at[b], lambda b, d: p.value_low.at[d], lambda b, d: p.value_low.at[d],
        me.y, me.at_y, *sems, 88)
    weight_z = [
        ReduceRing(
            lambda b, half, k=k: halves(p.weights.at[k, b], NL // 2, half), inbox(p.weights_in.at[k], NL // 2),
            me.z, *z, *sems, 96 + 8 * k)
        for k in range(2)
    ]
    return key_y, value_z, key_z, value_y, weight_z


def columns(c, place):
    return pl.ds(pl.multiple_of((c * NX + place) * COLS, COLS), COLS)


def rows_of(place):
    return pl.ds(pl.multiple_of(place * OWN, OWN), OWN)


class Swap:
    def __init__(self, me, p, queries, out_grad):
        self.me, self.p = me, p
        self.sent, self.own = [], []
        for c in range(2):
            for d in range(NX):
                to = lax.rem(me.xc + d, NX)
                for n, (src, dst) in enumerate(((queries, p.q_rows), (out_grad, p.g_rows))):
                    src_ref = src.at[:, columns(c, to)]
                    dst_ref = dst.at[c, rows_of(me.xc)]
                    if d == 0:
                        copy = pltpu.make_async_copy(src_ref, dst_ref, p.swap_own.at[n * 2 + c])
                        self.own.append(copy)
                    else:
                        sem = (d - 1) * 4 + n * 2 + c
                        copy = remote(src_ref, dst_ref, p.swap_send, p.swap_recv, sem, me.at_x(d))
                        self.sent.append(copy)
                    copy.start()

    def wait(self, c):
        me, p = self.me, self.p
        for d in range(1, NX):
            source = lax.rem(me.xc + (NX - d), NX)
            for n, dst in enumerate((p.q_rows, p.g_rows)):
                ref = dst.at[c, rows_of(source)]
                sem = (d - 1) * 4 + n * 2 + c
                remote(ref, ref, p.swap_send, p.swap_recv, sem, me.at_x(d)).wait_recv()
        for copy in self.own[c * 2:c * 2 + 2]:
            copy.wait()

    def finish(self):
        for copy in self.sent:
            copy.wait_send()


class SwapBack:
    def __init__(self, me, p, out):
        self.me, self.p, self.out = me, p, out
        self.sent, self.own = [], []
        for d in range(NX):
            to = lax.rem(me.xc + d, NX)
            for c in range(2):
                src_ref = p.grad_q.at[c, rows_of(to)]
                dst_ref = out.at[:, columns(c, me.xc)]
                if d == 0:
                    copy = pltpu.make_async_copy(src_ref, dst_ref, p.back_own.at[c])
                    self.own.append(copy)
                else:
                    copy = remote(src_ref, dst_ref, p.back_send, p.back_recv, (d - 1) * 2 + c, me.at_x(d))
                    self.sent.append(copy)
                copy.start()

    def finish(self):
        me, p = self.me, self.p
        for d in range(1, NX):
            source = lax.rem(me.xc + (NX - d), NX)
            for c in range(2):
                ref = self.out.at[:, columns(c, source)]
                remote(ref, ref, p.back_send, p.back_recv, (d - 1) * 2 + c, me.at_x(d)).wait_recv()
        for copy in self.own:
            copy.wait()
        for copy in self.sent:
            copy.wait_send()


def attend(me, p, s, h, t, c, entries, gate, gain):
    for e in range(LIST):
        rows = slice(e * LAT, (e + 1) * LAT)
        slot = entries[t][e][0]
        s.key_tile[rows, :] = p.keys[c * NL + lax.div(slot, NZ), lax.rem(slot, NZ)]
        s.value_tile[rows, :] = p.values[lax.rem(slot, NZ), c * NL + lax.div(slot, NZ)]
    kt = s.key_tile[...]
    vt = s.value_tile[...]
    base = t * TILE
    cols = slice(h * HD, (h + 1) * HD)
    q = s.q_rows[c, base:base + TILE, cols].astype(F32)
    g = s.g_rows[c, base:base + TILE, cols].astype(F32)
    inverse = lax.rsqrt(jnp.mean(q * q, axis=1, keepdims=True) + EPS)
    q_hat = (q * inverse * gain).astype(BF16)
    ctx = (gate * g).astype(BF16)
    scores = dot(kt, q_hat, 1, 1)
    grad_probs = dot(vt, ctx, 1, 1)
    token = me.seq * (2 * TOK) + me.yh * TOK + base + lax.broadcasted_iota(jnp.int32, (1, TILE), 1)
    total = jnp.zeros((1, TILE), F32)
    inner = jnp.zeros((1, TILE), F32)
    dead = jnp.ones((1, TILE), F32)
    exps = []
    for e in range(LIST):
        rows = slice(e * LAT, (e + 1) * LAT)
        live = entries[t][e][1] < token
        dead = jnp.where(live, 0.0, dead)
        x = jnp.where(live, jnp.exp2(scores[rows] * (SCALE * LOG2E)), 0.0)
        exps.append(x)
        total = total + jnp.sum(x, axis=0, keepdims=True)
        inner = inner + jnp.sum(x * grad_probs[rows], axis=0, keepdims=True)
    norm = 1.0 / (total + dead)
    inner = inner * norm
    probs = []
    grads = []
    for e in range(LIST):
        rows = slice(e * LAT, (e + 1) * LAT)
        prob = exps[e] * norm
        probs.append(prob.astype(BF16))
        grads.append((prob * (grad_probs[rows] - inner)).astype(BF16))
    probs = jnp.concatenate(probs, axis=0)
    grads = jnp.concatenate(grads, axis=0)
    s.key_sums[t, c, 0:LIST] = (dot(grads, q_hat, 1, 0) * SCALE).reshape(LIST, LAT, HD)
    s.value_sums[t, c, 0:LIST] = dot(probs, ctx, 1, 0).reshape(LIST, LAT, HD)
    up = dot(kt.T, grads, 1, 0).T * SCALE * gain
    row_inner = jnp.mean(up * q, axis=1, keepdims=True)
    s.grad_q[c, base:base + TILE, cols] = (inverse * (up - q * (inverse * inverse * row_inner))).astype(BF16)


def find_places(places, entries):
    def one_slot(slot, carry):
        for t in range(2):
            found = jnp.int32(LIST)
            for e in range(LIST):
                found = jnp.where(entries[t][e][2] == slot, e, found)
            places[t, slot] = found
        return carry

    lax.fori_loop(0, SLOTS, one_slot, 0)


def to_slots(tile_sums, places, target):
    def one_slot(slot, carry):
        for c in range(2):
            target(c, lax.div(slot, NZ), lax.rem(slot, NZ))[...] = (
                tile_sums[0, c, places[0, slot]] + tile_sums[1, c, places[1, slot]]).astype(BF16)
        return carry

    lax.fori_loop(0, SLOTS, one_slot, 0)


def kernel(
    tile_list, media_slot, media_position, gate_alpha,
    queries, out_grad, latents, key_weight, value_weight, query_gain, key_gain,
    out_queries, out_latents, out_key_weight, out_value_weight,
    *refs,
):
    count = len(PIECE)
    pieces = [Refs(PIECE, refs[h * count:(h + 1) * count]) for h in range(2)]
    s = Refs(SHARED, refs[2 * count:])
    me = Place()
    loads = [
        pltpu.make_async_copy(src, dst, s.load_sem.at[n])
        for n, (src, dst) in enumerate(
            ((latents, s.latents), (key_weight, s.key_weight), (value_weight, s.value_weight)))
    ]
    for load in loads:
        load.start()
    wait_for_all = greet(
        [me.at_y(d) for d in range(1, NY)]
        + [me.at_z(d) for d in range(1, NZ)]
        + [me.at_head(d) for d in range(1, 2 * NX)]
    )
    for load in loads:
        load.wait()

    gain_k = key_gain[...]
    flat = s.latents[...]
    s.raw[...] = jnp.dot(flat, s.key_weight[...], preferred_element_type=F32)
    own_values = jnp.dot(flat, s.value_weight[...], preferred_element_type=F32).astype(BF16)
    for h, p in enumerate(pieces):
        cols = slice(h * HD, (h + 1) * HD)
        part = s.raw[:, cols]
        inverse = lax.rsqrt(jnp.mean(part * part, axis=1, keepdims=True) + EPS)
        p.keys[me.y, me.z] = (part * inverse * gain_k).astype(BF16)
        p.values[me.z, me.y] = own_values[:, cols]

    wait_for_all()

    firsts, seconds = zip(*[gather_rings(me, p) for p in pieces])

    def start(rings, step):
        for ring in rings:
            ring.start(step)

    def follow(rings, step):
        for ring in rings:
            ring.wait(step)
            if step < 3:
                ring.start(step + 1)

    for rings in firsts:
        for ring in rings:
            ring.start()
    swap = Swap(me, s, queries, out_grad)

    entries = []
    for t in range(2):
        entries.append([])
        for e in range(LIST):
            image = tile_list[me.yh * 2 + t, e]
            held = jnp.maximum(image, 0)
            slot = media_slot[held]
            entries[t].append((
                slot,
                jnp.where(image >= 0, media_position[held], DEAD),
                jnp.where(image >= 0, slot, SLOTS),
            ))
    gate = jnp.tanh(jnp.full((1, HD), gate_alpha[0], F32))
    gain_q = query_gain[...]
    for t in range(2):
        for c in range(2):
            s.key_sums[t, c, LIST] = jnp.zeros((LAT, HD), F32)
            s.value_sums[t, c, LIST] = jnp.zeros((LAT, HD), F32)

    find_places(s.places, entries)
    s.latents_t[...] = flat.astype(F32).T.astype(BF16)

    for rings, later in zip(firsts, seconds):
        for ring in rings:
            for d in range(1, 8):
                ring.wait(d)
        start(later, 0)
    for step in range(3):
        follow(seconds[0], step)
        follow(seconds[1], step)
    follow(seconds[0], 3)

    units = [(t, c) for c in range(2) for t in range(2)]

    def run(h, n):
        t, c = units[n]
        attend(me, pieces[h], s, h, t, c, entries, gate, gain_q)

    swap.wait(0)
    run(0, 0)
    follow(seconds[1], 3)
    run(0, 1)
    swap.wait(1)
    run(0, 2)
    run(0, 3)
    sums = [reduce_rings(me, p) for p in pieces]
    raw_grads, value_grads, low_copies, head_copies = {}, {}, [], []

    def tasks(h):
        p = pieces[h]
        key_y, value_z, key_z, value_y, weight_z = sums[h]

        def begin():
            to_slots(s.key_sums, s.places, lambda c, low, z: p.grad_keys.at[c * NL + low, z])
            for ring in key_y:
                ring.start()
            to_slots(s.value_sums, s.places, lambda c, low, z: p.grad_values.at[z, c * NL + low])
            for ring in value_z:
                ring.start()

        def first(step):
            def act():
                for pair in zip(key_y, value_z):
                    for ring in pair:
                        ring.step(step)
            return act

        def turn():
            for n, ring in enumerate(key_y):
                p.key_mid[n * 4:n * 4 + 4] = ring.total().astype(BF16)
            key_z.start()
            for n, ring in enumerate(value_z):
                p.value_mid[n * 4:n * 4 + 4] = ring.total().astype(BF16)
            value_y.start()

        def own_image():
            key_sum = p.key_mid[me.z].astype(F32)
            for d in (1, 7, 2, 6, 3, 5, 4):
                key_sum = key_sum + key_z.wait(d)[...].astype(F32)
            value_sum = p.value_mid[me.y].astype(F32)
            for d in (1, 7, 2, 6, 3, 5, 4):
                value_sum = value_sum + value_y.wait(d)[...].astype(F32)
            part = s.raw[:, h * HD:(h + 1) * HD]
            inverse = lax.rsqrt(jnp.mean(part * part, axis=1, keepdims=True) + EPS)
            up = key_sum * gain_k
            row_inner = jnp.mean(up * part, axis=1, keepdims=True)
            raw_grads[h] = (inverse * (up - part * (inverse * inverse * row_inner))).astype(BF16)
            value_grads[h] = value_sum.astype(BF16)
            both = jnp.concatenate([raw_grads[h], value_grads[h]], axis=1)
            share = jnp.dot(s.latents_t[...], both, preferred_element_type=F32)
            for k in range(2):
                for n in range(SLOTS):
                    block = share[n * 40:(n + 1) * 40, k * HD:(k + 1) * HD]
                    block = jnp.concatenate([block, jnp.zeros((PAD - 40, HD), F32)], axis=0)
                    p.weights[k, n % NZ, n // NZ] = block.astype(BF16)
                weight_z[k].start()

        def third(step):
            def act():
                for ring in weight_z:
                    ring.step(step)
                if h == 1 and step == 1:
                    latent_share()
            return act

        def low():
            for k, ring in enumerate(weight_z):
                p.low_out[:, :, k * HD:(k + 1) * HD] = ring.total().astype(BF16)
            for d in range(1, NL):
                copy = remote(
                    p.low_out.at[lax.rem(me.yl + d, NL)], p.low_in.at[d], p.low_send, p.low_recv, d, me.at_low(d))
                copy.start()
                low_copies.append(copy)

        def last():
            total = p.low_out[me.yl].astype(F32)
            for d in range(1, NL):
                ref = p.low_in.at[d]
                remote(ref, ref, p.low_send, p.low_recv, d, me.at_low(d)).wait_recv()
                total = total + ref[...].astype(F32)
            cols = slice(h * HD, (h + 1) * HD)
            out_key_weight[:, cols] = total[0:40, 0:HD]
            out_value_weight[:, cols] = total[0:40, HD:]

        return (
            [begin] + [first(step) for step in (1, 2, 3)] + [turn, own_image]
            + [third(step) for step in (1, 2, 3)] + [low, last]
        )

    def latent_share():
        raw_grad = jnp.concatenate([raw_grads[0], raw_grads[1]], axis=1)
        value_grad = jnp.concatenate([value_grads[0], value_grads[1]], axis=1)
        s.wide[...] = dot(raw_grad, s.key_weight[...], 1, 1) + dot(value_grad, s.value_weight[...], 1, 1)
        s.spread[...] = jnp.zeros_like(s.spread)
        for d in range(2 * NX):
            for n in range(VD // HD):
                s.spread[d, 4 * n:4 * n + 4, :] = s.wide[4 * d:4 * d + 4, n * HD:(n + 1) * HD]
        s.shares[...] = s.spread[...].astype(BF16)
        for d in range(1, 2 * NX):
            copy = remote(
                s.shares.at[lax.rem(me.head + d, 2 * NX)], s.shares_in.at[d], s.head_send, s.head_recv, d,
                me.at_head(d))
            copy.start()
            head_copies.append(copy)

    left = [tasks(0), tasks(1)]

    def go(h):
        left[h].pop(0)()

    go(0)
    run(1, 0)
    run(1, 1)
    go(0)
    run(1, 2)
    run(1, 3)
    go(1)
    go(0)
    back = SwapBack(me, s, out_queries)
    while left[1]:
        go(1)
        if left[0]:
            go(0)

    total = s.shares[me.head].astype(F32)
    for d in range(1, 2 * NX):
        ref = s.shares_in.at[d]
        remote(ref, ref, s.head_send, s.head_recv, d, me.at_head(d)).wait_recv()
        total = total + ref[...].astype(F32)
    s.spread[0] = total
    for n in range(VD // HD):
        s.wide[0:4, n * HD:(n + 1) * HD] = s.spread[0, 4 * n:4 * n + 4, :]
    out_latents[...] = s.wide[0:4, :].astype(BF16)

    back.finish()
    swap.finish()
    for copy in head_copies + low_copies:
        copy.wait_send()
    for rings in firsts + seconds:
        for ring in rings:
            ring.finish()
    for key_y, value_z, key_z, value_y, weight_z in sums:
        for ring in key_y + value_z + [key_z, value_y] + weight_z:
            ring.finish()


def hand_on(*refs):
    for source, result in zip(refs[:4], refs[4:]):
        result[...] = source[...]


VMEM = pl.BlockSpec(memory_space=pltpu.VMEM)
SMEM = pl.BlockSpec(memory_space=pltpu.SMEM)
HBM = pl.BlockSpec(memory_space=pl.ANY)
LIMIT = 60 * 1024 * 1024


def struct(shape, dtype):
    return jax.ShapeDtypeStruct(shape, dtype)


def body(
    queries,
    out_grad,
    latents,
    key_weight,
    value_weight,
    query_gain,
    key_gain,
    gate_alpha,
    media_slot,
    media_position,
    tile_list,
):
    shapes = (
        struct((OWN, 2 * NX * COLS), BF16),
        struct((4, VD), BF16),
        struct((VD // SLOTS, COLS), F32),
        struct((VD // SLOTS, COLS), F32),
    )
    grads = pl.pallas_call(
        kernel,
        out_shape=shapes,
        in_specs=[SMEM] * 4 + [HBM] * 5 + [VMEM] * 2,
        out_specs=(HBM, VMEM, VMEM, VMEM),
        scratch_shapes=list(PIECE.values()) * 2 + list(SHARED.values()),
        compiler_params=pltpu.CompilerParams(collective_id=0, has_side_effects=True, vmem_limit_bytes=LIMIT),
        name="backward",
    )(
        tile_list, media_slot, media_position, gate_alpha,
        queries, out_grad, latents.reshape(LAT, VD), key_weight, value_weight,
        query_gain.reshape(1, HD), key_gain.reshape(1, HD),
    )
    query_grad, latent_grad, key_weight_grad, value_weight_grad = pl.pallas_call(
        hand_on,
        out_shape=shapes,
        in_specs=[VMEM] * 4,
        out_specs=(VMEM,) * 4,
        compiler_params=pltpu.CompilerParams(vmem_limit_bytes=LIMIT),
        name="hand_on",
    )(*grads)
    return (query_grad, latent_grad.reshape(1, 4, VD), key_weight_grad, value_weight_grad)


def solution(mesh):
    in_specs = (
        P(("seq", "head"), None),
        P(("seq", "head"), None),
        P("seq", None, None),
        P(None, "head"),
        P(None, "head"),
        P(),
        P(),
        P(),
        P(),
        P(),
        P("seq", None),
    )
    out_specs = (
        P(("seq", "head"), None),
        P("seq", "head", None),
        P("seq", "head"),
        P("seq", "head"),
    )
    return jax.shard_map(body, mesh=mesh, in_specs=in_specs, out_specs=out_specs, check_vma=False)
```

```python
import jax
import jax.numpy as jnp
from jax import lax
from jax.experimental import pallas as pl
from jax.experimental.pallas import tpu as pltpu
from jax.sharding import PartitionSpec as P

HD = 128
EPS = 1e-06
SCALE = HD ** (-0.5)
LOG2E = 1.4426950408889634
MESH = pl.DeviceIdType.MESH

NZ = 8
NL = 4
NY = 8
NX = 8
LAT = 64
LIST = 8
TILE = 512
TOK = 1024
OWN = 128
COLS = 256
VD = 1280
PAD = 48
SLOTS = 32
DEAD = 1 << 30

F32 = jnp.float32
BF16 = jnp.bfloat16


def dot(a, b, ca, cb):
    return lax.dot_general(a, b, (((ca,), (cb,)), ((), ())), preferred_element_type=F32)


class Place:
    def __init__(self):
        self.seq = lax.axis_index("seq")
        self.head = lax.axis_index("head")
        self.z = lax.rem(self.seq, NZ)
        self.yl = lax.div(self.seq, NZ)
        self.yh = lax.div(self.head, NX)
        self.xc = lax.rem(self.head, NX)
        self.y = self.yh * NL + self.yl

    def at_y(self, step):
        y = lax.rem(self.y + (step + NY), NY)
        return (lax.rem(y, NL) * NZ + self.z, lax.div(y, NL) * NX + self.xc)

    def at_z(self, step):
        z = lax.rem(self.z + (step + NZ), NZ)
        return (self.yl * NZ + z, self.head)

    def at_x(self, step):
        return (self.seq, self.yh * NX + lax.rem(self.xc + step, NX))

    def at_head(self, step):
        return (self.seq, lax.rem(self.head + step, 2 * NX))

    def at_low(self, step):
        return (lax.rem(self.yl + step, NL) * NZ + self.z, self.head)


def greet(partners):
    for partner in partners:
        pl.semaphore_signal(pltpu.get_barrier_semaphore(), inc=1, device_id=partner, device_id_type=MESH)
    return lambda: pl.semaphore_wait(pltpu.get_barrier_semaphore(), len(partners))


def remote(src, dst, sends, recvs, sem, device):
    return pltpu.make_async_remote_copy(
        src_ref=src,
        dst_ref=dst,
        send_sem=sends.at[sem],
        recv_sem=recvs.at[sem],
        device_id=device,
        device_id_type=MESH,
    )


class GatherRing:
    def __init__(self, block, me, right, left, sends, recvs, base):
        self.block, self.me, self.targets = block, me, (right, left)
        self.sends, self.recvs, self.base = sends, recvs, base
        self.started = []

    def copy(self, way, step, shift):
        offset = (-step - shift) if way == 0 else (step + shift)
        ref = self.block(lax.rem(self.me + (offset + 8), 8), way if step == 3 else None)
        return remote(ref, ref, self.sends, self.recvs, self.base + way * 4 + step, self.targets[way])

    def start(self, step, ways=(0, 1)):
        for way in ways:
            copy = self.copy(way, step, 0)
            copy.start()
            self.started.append(copy)

    def follow(self, step):
        for way in (0, 1):
            self.copy(way, step, 1).wait_recv()
            if step < 3:
                self.start(step + 1, (way,))

    def finish(self):
        for copy in self.started:
            copy.wait_send()


class Direct:
    def __init__(self, source, target, arrived, me, at, sends, recvs, base):
        self.source, self.target, self.arrived, self.me, self.at = source, target, arrived, me, at
        self.sends, self.recvs, self.base = sends, recvs, base
        self.started = []

    def start(self):
        for d in (4, 3, 5, 2, 6, 1, 7):
            index = lax.rem(self.me + d, 8)
            copy = remote(
                self.source(index), self.target(index, d), self.sends, self.recvs, self.base + d, self.at(d))
            copy.start()
            self.started.append(copy)

    def wait(self, d):
        ref = self.arrived(lax.rem(self.me + (8 - d), 8), d)
        remote(ref, ref, self.sends, self.recvs, self.base + d, self.at(d)).wait_recv()
        return ref

    def finish(self):
        for copy in self.started:
            copy.wait_send()


class ReduceRing:
    def __init__(self, own, inbox, me, right, left, sends, recvs, base):
        self.own, self.inbox, self.me, self.targets = own, inbox, me, (right, left)
        self.sends, self.recvs, self.base = sends, recvs, base
        self.started = []

    def index(self, way, step):
        offset = 4 - step if way == 0 else step + 4
        return lax.rem(self.me + offset, 8)

    def send(self, way, step, src):
        copy = remote(
            src, self.inbox(way, step), self.sends, self.recvs, self.base + way * 4 + step, self.targets[way]
        )
        copy.start()
        self.started.append(copy)

    def arrive(self, way, step):
        ref = self.inbox(way, step)
        remote(ref, ref, self.sends, self.recvs, self.base + way * 4 + step, self.targets[way]).wait_recv()

    def start(self):
        for way in (0, 1):
            self.send(way, 0, self.own(self.index(way, 0), way))

    def step(self, step):
        for way in (0, 1):
            self.arrive(way, step - 1)
            index = self.index(way, step)
            here = self.inbox(way, step - 1)
            if step == 1:
                part = self.own(index, way)
                part[...] = (part[...].astype(F32) + here[...].astype(F32)).astype(BF16)
                self.send(way, 1, self.own(index, None))
            else:
                here[...] = (here[...].astype(F32) + self.own(index, None)[...].astype(F32)).astype(BF16)
                self.send(way, step, here)

    def total(self):
        for way in (0, 1):
            self.arrive(way, 3)
        return (
            self.own(self.me, None)[...].astype(F32)
            + self.inbox(0, 3)[...].astype(F32)
            + self.inbox(1, 3)[...].astype(F32)
        )

    def finish(self):
        for copy in self.started:
            copy.wait_send()


def halves(ref, size, half):
    return ref if half is None else ref.at[pl.ds(half * size, size)]


def quarters(ref, part, half):
    return ref.at[pl.ds(part * 4, 4)] if half is None else ref.at[pl.ds(part * 4 + half * 2, 2)]


def scratch(*shape, dtype=BF16):
    return pltpu.VMEM(shape, dtype)


PIECE = dict(
    keys=scratch(NY, NZ, LAT, HD),
    values=scratch(NZ, NY, LAT, HD),
    grad_keys=scratch(NY, NZ, LAT, HD),
    grad_values=scratch(NZ, NY, LAT, HD),
    key_in=scratch(2, 2, 4, 4, LAT, HD),
    value_in=scratch(2, 2, 4, 4, LAT, HD),
    key_mid=scratch(NZ, LAT, HD),
    value_mid=scratch(NY, LAT, HD),
    key_low=scratch(NZ, LAT, HD),
    value_low=scratch(NY, LAT, HD),
    weights=scratch(NZ, NL, PAD, HD),
    weights_in=scratch(2, 4, NL, PAD, HD),
    low_out=scratch(NL, PAD, HD),
    low_in=scratch(NL, PAD, HD),
    wide_out=scratch(NL, NZ, PAD, HD),
    wide_in=scratch(NL, NZ, PAD, HD),
    line_out=scratch(NZ, PAD, HD),
    line_in=scratch(NZ, PAD, HD),
    wide_send=pltpu.SemaphoreType.DMA((4,)),
    wide_recv=pltpu.SemaphoreType.DMA((4,)),
    ring_send=pltpu.SemaphoreType.DMA((112,)),
    ring_recv=pltpu.SemaphoreType.DMA((112,)),
    low_send=pltpu.SemaphoreType.DMA((4,)),
    low_recv=pltpu.SemaphoreType.DMA((4,)),
)
SHARED = dict(
    q_rows=scratch(2, TOK, COLS),
    g_rows=scratch(2, TOK, COLS),
    grad_q=scratch(2, TOK, COLS),
    swap_send=pltpu.SemaphoreType.DMA((28,)),
    swap_recv=pltpu.SemaphoreType.DMA((28,)),
    swap_own=pltpu.SemaphoreType.DMA((4,)),
    back_send=pltpu.SemaphoreType.DMA((14,)),
    back_recv=pltpu.SemaphoreType.DMA((14,)),
    back_own=pltpu.SemaphoreType.DMA((2,)),
    latents=scratch(LAT, VD),
    key_weight=scratch(VD, COLS),
    value_weight=scratch(VD, COLS),
    raw=scratch(LAT, COLS, dtype=F32),
    key_tile=scratch(LIST * LAT, HD),
    value_tile=scratch(LIST * LAT, HD),
    key_sums=scratch(2, 2, LIST + 1, LAT, HD, dtype=F32),
    value_sums=scratch(2, 2, LIST + 1, LAT, HD, dtype=F32),
    shares=scratch(2 * NX, PAD, HD),
    shares_in=scratch(2 * NX, PAD, HD),
    spread=scratch(2 * NX, PAD, HD, dtype=F32),
    wide=scratch(LAT, VD, dtype=F32),
    latents_t=scratch(VD, LAT),
    places=pltpu.SMEM((2, SLOTS), jnp.int32),
    load_sem=pltpu.SemaphoreType.DMA((3,)),
    head_send=pltpu.SemaphoreType.DMA((16,)),
    head_recv=pltpu.SemaphoreType.DMA((16,)),
)


class Refs:
    def __init__(self, names, refs):
        self.__dict__.update(zip(names, refs))


def inbox(buffer, size):
    def place(way, step):
        ref = buffer.at[way, step]
        return ref.at[pl.ds(way * size, size)] if step == 0 else ref

    return place


def gather_rings(me, p):
    y, z = (me.at_y(1), me.at_y(-1)), (me.at_z(1), me.at_z(-1))
    sems = (p.ring_send, p.ring_recv)
    first = (
        Direct(
            lambda b: p.keys.at[me.y, me.z], lambda b, d: p.keys.at[me.y, me.z], lambda b, d: p.keys.at[me.y, b],
            me.z, me.at_z, *sems, 0),
        Direct(
            lambda b: p.values.at[me.z, me.y], lambda b, d: p.values.at[me.z, me.y],
            lambda b, d: p.values.at[me.z, b], me.y, me.at_y, *sems, 8),
    )
    second = []
    for n in range(2):
        second += [
            GatherRing(lambda b, half, n=n: quarters(p.keys.at[b], n, half), me.y, *y, *sems, 16 + 8 * n),
            GatherRing(lambda b, half, n=n: quarters(p.values.at[b], n, half), me.z, *z, *sems, 32 + 8 * n),
        ]
    return first, second


def reduce_rings(me, p):
    y, z = (me.at_y(1), me.at_y(-1)), (me.at_z(1), me.at_z(-1))
    sems = (p.ring_send, p.ring_recv)
    key_y = [
        ReduceRing(
            lambda b, half, n=n: quarters(p.grad_keys.at[b], n, half), inbox(p.key_in.at[n], 2),
            me.y, *y, *sems, 48 + 8 * n)
        for n in range(2)
    ]
    value_z = [
        ReduceRing(
            lambda b, half, n=n: quarters(p.grad_values.at[b], n, half), inbox(p.value_in.at[n], 2),
            me.z, *z, *sems, 64 + 8 * n)
        for n in range(2)
    ]
    key_z = Direct(
        lambda b: p.key_mid.at[b], lambda b, d: p.key_low.at[d], lambda b, d: p.key_low.at[d], me.z, me.at_z, *sems, 80)
    value_y = Direct(
        lambda b: p.value_mid.at[b], lambda b, d: p.value_low.at[d], lambda b, d: p.value_low.at[d],
        me.y, me.at_y, *sems, 88)
    weight_z = ReduceRing(
        lambda b, half: halves(p.weights.at[b], NL // 2, half), inbox(p.weights_in, NL // 2), me.z, *z, *sems, 96)
    line_z = Direct(
        lambda b: p.line_out.at[b], lambda b, d: p.line_in.at[d], lambda b, d: p.line_in.at[d],
        me.z, me.at_z, *sems, 104)
    return key_y, value_z, key_z, value_y, weight_z, line_z


def columns(c, place):
    return pl.ds(pl.multiple_of((c * NX + place) * COLS, COLS), COLS)


def rows_of(place):
    return pl.ds(pl.multiple_of(place * OWN, OWN), OWN)


class Swap:
    def __init__(self, me, p, queries, out_grad):
        self.me, self.p = me, p
        self.sent, self.own = [], []
        for c in range(2):
            for d in range(NX):
                to = lax.rem(me.xc + d, NX)
                for n, (src, dst) in enumerate(((queries, p.q_rows), (out_grad, p.g_rows))):
                    src_ref = src.at[:, columns(c, to)]
                    dst_ref = dst.at[c, rows_of(me.xc)]
                    if d == 0:
                        copy = pltpu.make_async_copy(src_ref, dst_ref, p.swap_own.at[n * 2 + c])
                        self.own.append(copy)
                    else:
                        sem = (d - 1) * 4 + n * 2 + c
                        copy = remote(src_ref, dst_ref, p.swap_send, p.swap_recv, sem, me.at_x(d))
                        self.sent.append(copy)
                    copy.start()

    def wait(self, c):
        me, p = self.me, self.p
        for d in range(1, NX):
            source = lax.rem(me.xc + (NX - d), NX)
            for n, dst in enumerate((p.q_rows, p.g_rows)):
                ref = dst.at[c, rows_of(source)]
                sem = (d - 1) * 4 + n * 2 + c
                remote(ref, ref, p.swap_send, p.swap_recv, sem, me.at_x(d)).wait_recv()
        for copy in self.own[c * 2:c * 2 + 2]:
            copy.wait()

    def finish(self):
        for copy in self.sent:
            copy.wait_send()


class SwapBack:
    def __init__(self, me, p, out):
        self.me, self.p, self.out = me, p, out
        self.sent, self.own = [], []
        for d in range(NX):
            to = lax.rem(me.xc + d, NX)
            for c in range(2):
                src_ref = p.grad_q.at[c, rows_of(to)]
                dst_ref = out.at[:, columns(c, me.xc)]
                if d == 0:
                    copy = pltpu.make_async_copy(src_ref, dst_ref, p.back_own.at[c])
                    self.own.append(copy)
                else:
                    copy = remote(src_ref, dst_ref, p.back_send, p.back_recv, (d - 1) * 2 + c, me.at_x(d))
                    self.sent.append(copy)
                copy.start()

    def finish(self):
        me, p = self.me, self.p
        for d in range(1, NX):
            source = lax.rem(me.xc + (NX - d), NX)
            for c in range(2):
                ref = self.out.at[:, columns(c, source)]
                remote(ref, ref, p.back_send, p.back_recv, (d - 1) * 2 + c, me.at_x(d)).wait_recv()
        for copy in self.own:
            copy.wait()
        for copy in self.sent:
            copy.wait_send()


def attend(me, p, s, h, t, c, entries, gate, gain):
    for e in range(LIST):
        rows = slice(e * LAT, (e + 1) * LAT)
        slot = entries[t][e][0]
        s.key_tile[rows, :] = p.keys[c * NL + lax.div(slot, NZ), lax.rem(slot, NZ)]
        s.value_tile[rows, :] = p.values[lax.rem(slot, NZ), c * NL + lax.div(slot, NZ)]
    kt = s.key_tile[...]
    vt = s.value_tile[...]
    base = t * TILE
    cols = slice(h * HD, (h + 1) * HD)
    q = s.q_rows[c, base:base + TILE, cols].astype(F32)
    g = s.g_rows[c, base:base + TILE, cols].astype(F32)
    inverse = lax.rsqrt(jnp.mean(q * q, axis=1, keepdims=True) + EPS)
    q_hat = (q * inverse * gain).astype(BF16)
    ctx = (gate * g).astype(BF16)
    scores = dot(kt, q_hat, 1, 1)
    grad_probs = dot(vt, ctx, 1, 1)
    token = me.seq * (2 * TOK) + me.yh * TOK + base + lax.broadcasted_iota(jnp.int32, (1, TILE), 1)
    total = jnp.zeros((1, TILE), F32)
    inner = jnp.zeros((1, TILE), F32)
    dead = jnp.ones((1, TILE), F32)
    exps = []
    for e in range(LIST):
        rows = slice(e * LAT, (e + 1) * LAT)
        live = entries[t][e][1] < token
        dead = jnp.where(live, 0.0, dead)
        x = jnp.where(live, jnp.exp2(scores[rows] * (SCALE * LOG2E)), 0.0)
        exps.append(x)
        total = total + jnp.sum(x, axis=0, keepdims=True)
        inner = inner + jnp.sum(x * grad_probs[rows], axis=0, keepdims=True)
    norm = 1.0 / (total + dead)
    inner = inner * norm
    probs = []
    grads = []
    for e in range(LIST):
        rows = slice(e * LAT, (e + 1) * LAT)
        prob = exps[e] * norm
        probs.append(prob.astype(BF16))
        grads.append((prob * (grad_probs[rows] - inner)).astype(BF16))
    probs = jnp.concatenate(probs, axis=0)
    grads = jnp.concatenate(grads, axis=0)
    s.key_sums[t, c, 0:LIST] = (dot(grads, q_hat, 1, 0) * SCALE).reshape(LIST, LAT, HD)
    s.value_sums[t, c, 0:LIST] = dot(probs, ctx, 1, 0).reshape(LIST, LAT, HD)
    up = dot(kt.T, grads, 1, 0).T * SCALE * gain
    row_inner = jnp.mean(up * q, axis=1, keepdims=True)
    s.grad_q[c, base:base + TILE, cols] = (inverse * (up - q * (inverse * inverse * row_inner))).astype(BF16)


def find_places(places, entries):
    def one_slot(slot, carry):
        for t in range(2):
            found = jnp.int32(LIST)
            for e in range(LIST):
                found = jnp.where(entries[t][e][2] == slot, e, found)
            places[t, slot] = found
        return carry

    lax.fori_loop(0, SLOTS, one_slot, 0)


def to_slots(tile_sums, places, target):
    def one_slot(slot, carry):
        for c in range(2):
            target(c, lax.div(slot, NZ), lax.rem(slot, NZ))[...] = (
                tile_sums[0, c, places[0, slot]] + tile_sums[1, c, places[1, slot]]).astype(BF16)
        return carry

    lax.fori_loop(0, SLOTS, one_slot, 0)


def kernel(
    tile_list, media_slot, media_position, gate_alpha,
    queries, out_grad, latents, key_weight, value_weight, query_gain, key_gain,
    out_queries, out_latents, out_key_weight, out_value_weight,
    *refs,
):
    count = len(PIECE)
    pieces = [Refs(PIECE, refs[h * count:(h + 1) * count]) for h in range(2)]
    s = Refs(SHARED, refs[2 * count:])
    me = Place()
    loads = [
        pltpu.make_async_copy(src, dst, s.load_sem.at[n])
        for n, (src, dst) in enumerate(
            ((latents, s.latents), (key_weight, s.key_weight), (value_weight, s.value_weight)))
    ]
    for load in loads:
        load.start()
    wait_for_all = greet(
        [me.at_y(d) for d in range(1, NY)]
        + [me.at_z(d) for d in range(1, NZ)]
        + [me.at_head(d) for d in range(1, 2 * NX)]
    )
    for load in loads:
        load.wait()

    gain_k = key_gain[...]
    flat = s.latents[...]
    s.raw[...] = jnp.dot(flat, s.key_weight[...], preferred_element_type=F32)
    own_values = jnp.dot(flat, s.value_weight[...], preferred_element_type=F32).astype(BF16)
    for h, p in enumerate(pieces):
        cols = slice(h * HD, (h + 1) * HD)
        part = s.raw[:, cols]
        inverse = lax.rsqrt(jnp.mean(part * part, axis=1, keepdims=True) + EPS)
        p.keys[me.y, me.z] = (part * inverse * gain_k).astype(BF16)
        p.values[me.z, me.y] = own_values[:, cols]

    wait_for_all()

    firsts, seconds = zip(*[gather_rings(me, p) for p in pieces])

    def start(rings, step):
        for ring in rings:
            ring.start(step)

    def follow(rings, step):
        for ring in rings:
            ring.follow(step)

    for rings in firsts:
        for ring in rings:
            ring.start()
    swap = Swap(me, s, queries, out_grad)

    entries = []
    for t in range(2):
        entries.append([])
        for e in range(LIST):
            image = tile_list[me.yh * 2 + t, e]
            held = jnp.maximum(image, 0)
            slot = media_slot[held]
            entries[t].append((
                slot,
                jnp.where(image >= 0, media_position[held], DEAD),
                jnp.where(image >= 0, slot, SLOTS),
            ))
    gate = jnp.tanh(jnp.full((1, HD), gate_alpha[0], F32))
    gain_q = query_gain[...]
    for t in range(2):
        for c in range(2):
            s.key_sums[t, c, LIST] = jnp.zeros((LAT, HD), F32)
            s.value_sums[t, c, LIST] = jnp.zeros((LAT, HD), F32)

    find_places(s.places, entries)
    s.latents_t[...] = flat.astype(F32).T.astype(BF16)

    for rings, later in zip(firsts, seconds):
        for ring in rings:
            for d in range(1, 8):
                ring.wait(d)
        start(later, 0)
    for step in range(3):
        follow(seconds[0], step)
        follow(seconds[1], step)
    follow(seconds[0], 3)

    units = [(t, c) for c in range(2) for t in range(2)]

    def run(h, n):
        t, c = units[n]
        attend(me, pieces[h], s, h, t, c, entries, gate, gain_q)

    swap.wait(0)
    run(0, 0)
    follow(seconds[1], 3)
    run(0, 1)
    swap.wait(1)
    run(0, 2)
    run(0, 3)
    sums = [reduce_rings(me, p) for p in pieces]
    raw_grads, value_grads, low_copies, head_copies = {}, {}, [], []

    def tasks(h):
        p = pieces[h]
        key_y, value_z, key_z, value_y, weight_z, line_z = sums[h]

        def begin():
            to_slots(s.key_sums, s.places, lambda c, low, z: p.grad_keys.at[c * NL + low, z])
            for ring in key_y:
                ring.start()
            to_slots(s.value_sums, s.places, lambda c, low, z: p.grad_values.at[z, c * NL + low])
            for ring in value_z:
                ring.start()

        def first(step):
            def act():
                for pair in zip(key_y, value_z):
                    for ring in pair:
                        ring.step(step)
            return act

        def turn():
            for n, ring in enumerate(key_y):
                p.key_mid[n * 4:n * 4 + 4] = ring.total().astype(BF16)
            key_z.start()
            for n, ring in enumerate(value_z):
                p.value_mid[n * 4:n * 4 + 4] = ring.total().astype(BF16)
            value_y.start()

        def own_image():
            key_sum = p.key_mid[me.z].astype(F32)
            for d in (1, 7, 2, 6, 3, 5, 4):
                key_sum = key_sum + key_z.wait(d)[...].astype(F32)
            value_sum = p.value_mid[me.y].astype(F32)
            for d in (1, 7, 2, 6, 3, 5, 4):
                value_sum = value_sum + value_y.wait(d)[...].astype(F32)
            part = s.raw[:, h * HD:(h + 1) * HD]
            inverse = lax.rsqrt(jnp.mean(part * part, axis=1, keepdims=True) + EPS)
            up = key_sum * gain_k
            row_inner = jnp.mean(up * part, axis=1, keepdims=True)
            raw_grads[h] = (inverse * (up - part * (inverse * inverse * row_inner))).astype(BF16)
            value_grads[h] = value_sum.astype(BF16)
            both = jnp.concatenate([raw_grads[h], value_grads[h]], axis=1)
            share = jnp.dot(s.latents_t[...], both, preferred_element_type=F32)
            for k in (1, 0):
                for n in range(SLOTS):
                    block = share[n * 40:(n + 1) * 40, k * HD:(k + 1) * HD]
                    block = jnp.concatenate([block, jnp.zeros((PAD - 40, HD), F32)], axis=0).astype(BF16)
                    if k == 0:
                        p.weights[n % NZ, n // NZ] = block
                    else:
                        p.wide_out[n // NZ, n % NZ] = block
                if k == 0:
                    weight_z.start()
                else:
                    to_low(p.wide_out, p.wide_in, p.wide_send, p.wide_recv)

        def to_low(out, place, sends, recvs):
            for d in (2, 1, 3):
                copy = remote(out.at[lax.rem(me.yl + d, NL)], place.at[d], sends, recvs, d, me.at_low(d))
                copy.start()
                low_copies.append(copy)

        def from_low(out, place, sends, recvs):
            total = out[me.yl].astype(F32)
            for d in (1, 3, 2):
                ref = place.at[d]
                remote(ref, ref, sends, recvs, d, me.at_low(d)).wait_recv()
                total = total + ref[...].astype(F32)
            return total

        def third(step):
            def act():
                weight_z.step(step)
                if step == 3:
                    p.line_out[...] = from_low(p.wide_out, p.wide_in, p.wide_send, p.wide_recv).astype(BF16)
                    line_z.start()
                if h == 1 and step == 1:
                    latent_share()
            return act

        def low():
            p.low_out[...] = weight_z.total().astype(BF16)
            to_low(p.low_out, p.low_in, p.low_send, p.low_recv)

        def last():
            cols = slice(h * HD, (h + 1) * HD)
            total = p.line_out[me.z].astype(F32)
            for d in (1, 7, 2, 6, 3, 5, 4):
                total = total + line_z.wait(d)[...].astype(F32)
            out_value_weight[:, cols] = total[0:40]
            out_key_weight[:, cols] = from_low(p.low_out, p.low_in, p.low_send, p.low_recv)[0:40]

        return (
            [begin] + [first(step) for step in (1, 2, 3)] + [turn, own_image]
            + [third(step) for step in (1, 2, 3)] + [low, last]
        )

    def latent_share():
        raw_grad = jnp.concatenate([raw_grads[0], raw_grads[1]], axis=1)
        value_grad = jnp.concatenate([value_grads[0], value_grads[1]], axis=1)
        s.wide[...] = dot(raw_grad, s.key_weight[...], 1, 1) + dot(value_grad, s.value_weight[...], 1, 1)
        s.spread[...] = jnp.zeros_like(s.spread)
        for d in range(2 * NX):
            for n in range(VD // HD):
                s.spread[d, 4 * n:4 * n + 4, :] = s.wide[4 * d:4 * d + 4, n * HD:(n + 1) * HD]
        s.shares[...] = s.spread[...].astype(BF16)
        for d in range(1, 2 * NX):
            copy = remote(
                s.shares.at[lax.rem(me.head + d, 2 * NX)], s.shares_in.at[d], s.head_send, s.head_recv, d,
                me.at_head(d))
            copy.start()
            head_copies.append(copy)

    left = [tasks(0), tasks(1)]

    def go(h):
        left[h].pop(0)()

    go(0)
    run(1, 0)
    run(1, 1)
    go(0)
    run(1, 2)
    run(1, 3)
    go(1)
    go(0)
    back = SwapBack(me, s, out_queries)
    while left[1]:
        go(1)
        if left[0]:
            go(0)

    total = s.shares[me.head].astype(F32)
    for d in range(1, 2 * NX):
        ref = s.shares_in.at[d]
        remote(ref, ref, s.head_send, s.head_recv, d, me.at_head(d)).wait_recv()
        total = total + ref[...].astype(F32)
    s.spread[0] = total
    for n in range(VD // HD):
        s.wide[0:4, n * HD:(n + 1) * HD] = s.spread[0, 4 * n:4 * n + 4, :]
    out_latents[...] = s.wide[0:4, :].astype(BF16)

    back.finish()
    swap.finish()
    for copy in head_copies + low_copies:
        copy.wait_send()
    for rings in firsts + seconds:
        for ring in rings:
            ring.finish()
    for key_y, value_z, key_z, value_y, weight_z, line_z in sums:
        for ring in key_y + value_z + [key_z, value_y, weight_z, line_z]:
            ring.finish()


def hand_on(*refs):
    for source, result in zip(refs[:4], refs[4:]):
        result[...] = source[...]


VMEM = pl.BlockSpec(memory_space=pltpu.VMEM)
SMEM = pl.BlockSpec(memory_space=pltpu.SMEM)
HBM = pl.BlockSpec(memory_space=pl.ANY)
LIMIT = 60 * 1024 * 1024


def struct(shape, dtype):
    return jax.ShapeDtypeStruct(shape, dtype)


def body(
    queries,
    out_grad,
    latents,
    key_weight,
    value_weight,
    query_gain,
    key_gain,
    gate_alpha,
    media_slot,
    media_position,
    tile_list,
):
    shapes = (
        struct((OWN, 2 * NX * COLS), BF16),
        struct((4, VD), BF16),
        struct((VD // SLOTS, COLS), F32),
        struct((VD // SLOTS, COLS), F32),
    )
    grads = pl.pallas_call(
        kernel,
        out_shape=shapes,
        in_specs=[SMEM] * 4 + [HBM] * 5 + [VMEM] * 2,
        out_specs=(HBM, VMEM, VMEM, VMEM),
        scratch_shapes=list(PIECE.values()) * 2 + list(SHARED.values()),
        compiler_params=pltpu.CompilerParams(collective_id=0, has_side_effects=True, vmem_limit_bytes=LIMIT),
        name="backward",
    )(
        tile_list, media_slot, media_position, gate_alpha,
        queries, out_grad, latents.reshape(LAT, VD), key_weight, value_weight,
        query_gain.reshape(1, HD), key_gain.reshape(1, HD),
    )
    query_grad, latent_grad, key_weight_grad, value_weight_grad = pl.pallas_call(
        hand_on,
        out_shape=shapes,
        in_specs=[VMEM] * 4,
        out_specs=(VMEM,) * 4,
        compiler_params=pltpu.CompilerParams(vmem_limit_bytes=LIMIT),
        name="hand_on",
    )(*grads)
    return (query_grad, latent_grad.reshape(1, 4, VD), key_weight_grad, value_weight_grad)


def solution(mesh):
    in_specs = (
        P(("seq", "head"), None),
        P(("seq", "head"), None),
        P("seq", None, None),
        P(None, "head"),
        P(None, "head"),
        P(),
        P(),
        P(),
        P(),
        P(),
        P("seq", None),
    )
    out_specs = (
        P(("seq", "head"), None),
        P("seq", "head", None),
        P("seq", "head"),
        P("seq", "head"),
    )
    return jax.shard_map(body, mesh=mesh, in_specs=in_specs, out_specs=out_specs, check_vma=False)
```
